512 devices in a mesh: gx: 16 (over x, z_lo), gy: 8 (over y, core), gz: 4 (over z_hi).
Axes of the slice: x: 4, y: 4, z: 16 (z_hi: 4, z_lo: 4; z = z_hi * 4 + z_lo), core: 2. Of those that a mesh axis runs over, the one named last changes fastest.
Arguments:
- velocity: float32 [3, 256, 256, 512], P(None, 'gx', 'gy', 'gz'), may hold values from -6 to 6
- nut_field: float32 [256, 256, 512], P('gx', 'gy', 'gz'), may hold values from 0.03 to 0.1
- bar_velocity: float32 [3, 256, 256, 512], P(None, 'gx', 'gy', 'gz'), may hold values from -0.3125 to 0.3125
- bar_nut: float32 [256, 256, 512], P('gx', 'gy', 'gz'), may hold values from -6 to 6
- wall_bin: int32 [256, 256, 512], P('gx', 'gy', 'gz'), may hold values from 0 to 31
- fluid_mask: int32 [256, 256, 512], P('gx', 'gy', 'gz'), may hold values 0 or 1
- dist_table: float32 [32], replicated, may hold values from 0.05 to 4
Outputs:
- bar_velocity_in: float32 [3, 256, 256, 512], P(None, 'gx', 'gy', 'gz')
- bar_nut_in: float32 [256, 256, 512], P('gx', 'gy', 'gz')
The draws below stay inside these ranges and needn't reach their ends.
All inputs are finite; a program needn't handle non-finite values. No bound on the sum of `fluid_mask` on one device may be relied on, other than what follows from the above.
Results may differ from the reference program's by a relative error of at most 0.0003.
Values sent between devices are 32-bit elements; how exact they have to be, the bound alone decides.
A program may use at most 128 MiB of HBM per device.

```python
import math
import jax
import jax.numpy as jnp
from jax import lax

CX = 16
NB = 32
NX = 256
NY = 256
NZ = 512


def with_ends(drawn, own_key, least, high):
    extent = drawn.shape
    index_at = [jax.random.randint(jax.random.fold_in(own_key, axis), (), 0, extent[axis]) for axis in range(len(extent))]
    drawn = drawn.at[tuple(index_at)].set(least)
    longest = extent.index(max(extent))
    index_at[longest] = (index_at[longest] + 1) % extent[longest]
    return drawn.at[tuple(index_at)].set(high)


def levels(rng, extent, shards, smallest, top_value):
    def one(axis_at, shards_of):
        draws = jax.random.uniform(jax.random.fold_in(jax.random.fold_in(rng, 6), axis_at), (shards_of,), jnp.float32, smallest / len(shards), top_value / len(shards))
        return jnp.repeat(jnp.exp(draws), extent[axis_at] // shards_of).reshape((-1,) + (1,) * (len(extent) - axis_at - 1))

    factor_of = one(*shards[0])
    for cut in shards[1:]:
        factor_of = factor_of * one(*cut)
    return factor_of


def normal_values(stream_key, extent, deviation, limit, pieces=(), kind=jnp.bfloat16):
    loudness = levels(stream_key, extent, pieces, -0.22, 0.18) if pieces else 1.0
    drawn = jax.random.normal(stream_key, extent, jnp.float32) * deviation * loudness
    return jnp.minimum(jnp.maximum(drawn, -limit), limit).astype(kind)


def setup_inputs(seed: int = 0) -> dict:
    splits = jax.random.split(jax.random.key(seed), 8)
    velocity = normal_values(splits[0], (3, NX, NY, NZ), 1.0, 6.0, ((1, 16), (2, 8), (3, 4)), jnp.float32)
    nut_field = jnp.clip(jnp.exp(math.log(0.1) - 1.2039728 * jax.random.uniform(splits[1], (NX, NY, NZ), jnp.float32) ** levels(splits[1], (NX, NY, NZ), ((0, 16), (1, 8), (2, 4)), -0.2, 0.2)), 0.03, 0.1)
    bar_velocity = normal_values(splits[2], (3, NX, NY, NZ), 0.05, 0.3125, ((1, 16), (2, 8), (3, 4)), jnp.float32)
    bar_nut = normal_values(splits[3], (NX, NY, NZ), 1.0, 6.0, ((0, 16), (1, 8), (2, 4)), jnp.float32)
    wall_bin = with_ends(jax.random.randint(splits[4], (NX, NY, NZ), 0, NB), jax.random.fold_in(splits[4], 1), 0, NB - 1).astype(jnp.int32)
    fluid_mask = with_ends((jax.random.randint(splits[5], (NX, NY, NZ), 0, 8) < 7).astype(jnp.int32), jax.random.fold_in(splits[5], 1), 0, 1)
    dist_table = jnp.clip(jnp.exp(jax.random.uniform(splits[6], (NB,), jnp.float32, math.log(0.05), math.log(4.0))), 0.05, 4.0)
    return {"velocity": velocity, "nut_field": nut_field, "bar_velocity": bar_velocity, "bar_nut": bar_nut, "wall_bin": wall_bin, "fluid_mask": fluid_mask, "dist_table": dist_table}


des_length = 0.65
step_size = 0.25
kappa_sq = 0.1681
coef_prod = 0.1355
coef_dest = 3.239

def gradient(padded):
    along_x = (padded[:, 2:, 1:-1, 1:-1] - padded[:, :-2, 1:-1, 1:-1]) * 0.5
    along_y = (padded[:, 1:-1, 2:, 1:-1] - padded[:, 1:-1, :-2, 1:-1]) * 0.5
    along_z = (padded[:, 1:-1, 1:-1, 2:] - padded[:, 1:-1, 1:-1, :-2]) * 0.5
    return jnp.stack([along_x, along_y, along_z], 1)

def transpose_grad(extended):
    part_x = (extended[:, 0, :-2, 1:-1, 1:-1] - extended[:, 0, 2:, 1:-1, 1:-1]) * 0.5
    part_y = (extended[:, 1, 1:-1, :-2, 1:-1] - extended[:, 1, 1:-1, 2:, 1:-1]) * 0.5
    part_z = (extended[:, 2, 1:-1, 1:-1, :-2] - extended[:, 2, 1:-1, 1:-1, 2:]) * 0.5
    return part_x + part_y + part_z

def local_section(fields, grads, inv_dist, mask):
    vel = fields[:3]
    nut = fields[3]
    tensor = grads[:3]
    spin = 0.5 * (tensor - jnp.swapaxes(tensor, 0, 1))
    omega = jnp.sqrt(1.0 + 2.0 * lax.optimization_barrier(jnp.sum(spin * spin, axis=(0, 1))))
    convect = lax.optimization_barrier(jnp.sum(tensor * vel[None], axis=1))
    new_vel = vel - step_size * mask * convect
    stilde = omega + nut * inv_dist * inv_dist / kappa_sq
    produce = coef_prod * stilde * nut
    destroy = coef_dest * (nut * inv_dist) ** 2
    advect = lax.optimization_barrier(jnp.sum(vel * grads[3], axis=0))
    new_nut = nut + step_size * mask * (produce - destroy - advect)
    return jnp.concatenate([new_vel, new_nut[None]], 0)

def section_adjoint(fields, grads, inv_dist, mask, bar_out):
    unused, pull = jax.vjp(lambda first, second: local_section(first, second, inv_dist, mask), fields, grads)
    return pull(bar_out)

def adjoint_block(big):
    fields_ext = big[:4]
    grads_ext = gradient(fields_ext)
    rest = big[4:, 1:-1, 1:-1, 1:-1]
    bar_local, bar_grads = section_adjoint(fields_ext[:, 1:-1, 1:-1, 1:-1], grads_ext, rest[4], rest[5], rest[:4])
    return bar_local[:, 1:-1, 1:-1, 1:-1] + transpose_grad(bar_grads)

def reference(velocity, nut_field, bar_velocity, bar_nut, wall_bin, fluid_mask, dist_table):
    fields = jnp.concatenate([velocity, nut_field[None]], 0)
    bars = jnp.concatenate([bar_velocity, bar_nut[None]], 0)
    inv_dist = 1.0 / jnp.minimum(dist_table[wall_bin], des_length)
    mask = fluid_mask.astype(jnp.float32)
    aux = jnp.concatenate([fields, bars, inv_dist[None], mask[None]], 0)
    padded = jnp.pad(aux, ((0, 0), (2, 2), (2, 2), (2, 2)))
    slabs = NX // CX

    def one_slab(index):
        start = (index * CX).astype(jnp.int32)
        block = lax.dynamic_slice_in_dim(padded, start, CX + 4, 1)
        return adjoint_block(block)
    result = lax.map(one_slab, jnp.arange(slabs, dtype=jnp.int32))
    result = jnp.transpose(result, (1, 0, 2, 3, 4)).reshape(4, NX, NY, NZ)
    return (result[:3], result[3])
```

```python
import functools

import jax
import jax.numpy as jnp
from jax import lax
from jax.experimental import pallas as pl
from jax.experimental.pallas import tpu as pltpu
from jax.sharding import PartitionSpec as P

des_length = 0.65
step_size = 0.25
kappa_sq = 0.1681
coef_prod = 0.1355
coef_dest = 3.239

MESH = pl.DeviceIdType.MESH
AXES = ("gx", "gy", "gz")
PAD = 8
LANES = 128


def section_kernel(
    counts, vel, nut, bvel, bnut, bins, mask, dist, ovel, onut,
    q, bar, bin_v, mask_v, nx, ny, res, comb, edge_t, y_halo, z_send, z_recv,
    w_send, w_recv, load_sem, store_sem, send_sem, recv_sem,
):
    cx, cy = nut.shape[0], nut.shape[1]
    tiles = cy // 8
    group = LANES // cy
    groups = cx // group
    rows = pl.ds(PAD, cy)
    planes = pl.ds(1, cx)
    f32 = jnp.float32

    pos = [lax.axis_index(a) for a in AXES]
    has = [(pos[d] > 0, pos[d] < counts[d] - 1) for d in range(3)]
    peer = [({AXES[d]: pos[d] - 1}, {AXES[d]: pos[d] + 1}) for d in range(3)]

    barrier = pltpu.get_barrier_semaphore()
    for d in range(3):
        for s in range(2):
            @pl.when(has[d][s])
            def _():
                pl.semaphore_signal(barrier, inc=1, device_id=peer[d][s], device_id_type=MESH)

    loads = [
        pltpu.make_async_copy(vel, q.at[0:3, planes, rows, :], load_sem.at[0]),
        pltpu.make_async_copy(nut, q.at[3, planes, rows, :], load_sem.at[1]),
        pltpu.make_async_copy(bvel, bar.at[0:3], load_sem.at[2]),
        pltpu.make_async_copy(bnut, bar.at[3], load_sem.at[3]),
        pltpu.make_async_copy(mask, mask_v, load_sem.at[4]),
        pltpu.make_async_copy(bins, bin_v, load_sem.at[5]),
    ]
    for copy in loads:
        copy.start()

    def remote(src, dst, slot, d, s):
        return pltpu.make_async_remote_copy(
            src_ref=src, dst_ref=dst, send_sem=send_sem.at[slot], recv_sem=recv_sem.at[slot],
            device_id=peer[d][s], device_id_type=MESH,
        )

    first = [[None, None] for _ in range(3)]
    for s in range(2):
        end = (0, cx - 1)[s]
        halo = (cx + 1, 0)[s]
        first[0][s] = [
            remote(vel.at[:, end], q.at[0:3, halo, rows, :], 0 + s, 0, s),
            remote(nut.at[end], q.at[3, halo, rows, :], 2 + s, 0, s),
        ]
        end = (0, cy - 1)[s]
        halo = (PAD + cy, PAD - 1)[s]
        first[1][s] = [
            remote(vel.at[:, :, end, :], q.at[0:3, planes, halo, :], 4 + s, 1, s),
            remote(nut.at[:, end, :], q.at[3, planes, halo, :], 6 + s, 1, s),
        ]
        first[2][s] = [remote(z_send.at[s], z_recv.at[1 - s], 8 + s, 2, s)]
    second = [[None, None] for _ in range(3)]
    for s in range(2):
        end = (1, cx)[s]
        halo = (cx + 1, 0)[s]
        second[0][s] = [remote(nx.at[:, end], nx.at[:, halo], 10 + s, 0, s)]
        end = (PAD, PAD + cy - 1)[s]
        second[1][s] = [remote(ny.at[:, :, end, :], y_halo.at[1 - s], 12 + s, 1, s)]
        second[2][s] = [remote(w_send.at[s], w_recv.at[1 - s], 14 + s, 2, s)]

    def start(copies, d):
        for s in range(2):
            @pl.when(has[d][s])
            def _():
                for copy in copies[d][s]:
                    copy.start()

    def arrive(copies, d):
        for s in range(2):
            @pl.when(has[d][1 - s])
            def _():
                for copy in copies[d][s]:
                    copy.wait_recv()

    def sent(copies, d):
        for s in range(2):
            @pl.when(has[d][s])
            def _():
                for copy in copies[d][s]:
                    copy.wait_send()

    for s in range(2):
        @pl.when(jnp.logical_not(has[0][s]))
        def _():
            halo = (0, cx + 1)[s]
            q[:, halo, rows, :] = jnp.zeros((4, cy, LANES), f32)
            nx[:, halo] = jnp.zeros((4, cy, LANES), f32)

        @pl.when(jnp.logical_not(has[1][s]))
        def _():
            halo = (PAD - 1, PAD + cy)[s]
            for f in range(4):
                q[f, planes, halo, :] = jnp.zeros((cx, LANES), f32)
            y_halo[s] = jnp.zeros((4, cx, LANES), f32)

        @pl.when(jnp.logical_not(has[2][s]))
        def _():
            z_recv[s] = jnp.zeros((4 * groups, LANES), f32)
            w_recv[s] = jnp.zeros((4 * groups, LANES), f32)

    present = sum(h.astype(jnp.int32) for pair in has for h in pair)
    pl.semaphore_wait(barrier, present)
    start(first, 0)
    start(first, 1)

    lane = lax.broadcasted_iota(jnp.int32, (8, LANES), 1)
    low = lane == 0
    high = lane == LANES - 1
    pairs = [lane < 2 * f + 2 for f in range(3)]

    def merge(parts):
        rolled = [pltpu.roll(part, 2 * f + 1, 1) for f, part in enumerate(parts)]
        out = rolled[3]
        for f in (2, 1, 0):
            out = jnp.where(pairs[f], rolled[f], out)
        return out

    def pack(dst):
        for g in range(groups):
            turned = comb[g * group:(g + 1) * group].reshape(LANES, LANES).T
            for f in range(4):
                dst[1, f * groups + g:f * groups + g + 1, :] = turned[2 * f:2 * f + 1]
                dst[0, f * groups + g:f * groups + g + 1, :] = turned[2 * f + 1:2 * f + 2]

    def unpack(src, sign):
        for g in range(groups):
            parts = []
            for f in range(4):
                parts.append(src[0, f * groups + g:f * groups + g + 1, :] * sign)
                parts.append(src[1, f * groups + g:f * groups + g + 1, :])
            parts.append(jnp.zeros((LANES - 8, LANES), f32))
            turned = jnp.concatenate(parts, axis=0).T
            edge_t[g * group:(g + 1) * group] = turned.reshape(group, cy, LANES)

    def halo_lanes(edges, f):
        return pltpu.roll(edges, LANES - (2 * f + 1), 1)

    loads[0].wait()
    loads[1].wait()

    def pack_plane(p, carry):
        for t in range(tiles):
            comb[p, 8 * t:8 * t + 8, :] = merge(
                [q[f, p + 1, PAD + 8 * t:PAD + 8 * t + 8, :] for f in range(4)]
            )
        return carry

    lax.fori_loop(0, cx, pack_plane, 0)
    pack(z_send)
    start(first, 2)

    for copy in loads[2:]:
        copy.wait()
    table = 1.0 / jnp.minimum(dist[...], des_length)
    table = table * table * (2.0 * (2.0 * coef_prod / kappa_sq - 2.0 * coef_dest))
    table = jnp.broadcast_to(
        jnp.pad(table, (0, LANES - table.shape[0])).reshape(1, LANES), (8, LANES)
    )

    for d in range(3):
        arrive(first, d)
    unpack(z_recv, 1.0)

    half = 0.5 * step_size

    def plane(p, carry):
        for t in range(tiles):
            lo = 8 * t
            mid = slice(PAD + lo, PAD + lo + 8)
            up = slice(PAD + lo + 1, PAD + lo + 9)
            down = slice(PAD + lo - 1, PAD + lo + 7)
            here = slice(lo, lo + 8)
            edges = edge_t[p, here, :]
            cell = [q[f, p + 1, mid, :] for f in range(4)]
            diff = []
            for f in range(4):
                ends = halo_lanes(edges, f)
                along_z = pltpu.roll(jnp.where(low, ends, cell[f]), LANES - 1, 1) - pltpu.roll(
                    jnp.where(high, ends, cell[f]), 1, 1
                )
                diff.append([
                    q[f, p + 2, mid, :] - q[f, p, mid, :],
                    q[f, p + 1, up, :] - q[f, p + 1, down, :],
                    along_z,
                ])
            wet = jnp.where(mask_v[p, here, :] != 0, half, 0.0)
            bars = [bar[i, p, here, :] for i in range(4)]
            scaled = [wet * b for b in bars]
            spin = {
                (0, 1): diff[0][1] - diff[1][0],
                (0, 2): diff[0][2] - diff[2][0],
                (1, 2): diff[1][2] - diff[2][1],
            }
            total = 1.0 + 0.25 * (
                spin[0, 1] * spin[0, 1] + spin[0, 2] * spin[0, 2] + spin[1, 2] * spin[1, 2]
            )
            inverse = lax.rsqrt(total)
            omega = total * inverse
            weight = scaled[3] * cell[3] * inverse * (0.5 * coef_prod)
            turn = {key: weight * value for key, value in spin.items()}
            flux = [[scaled[i] * cell[j] for j in range(3)] for i in range(4)]
            for (i, j), value in turn.items():
                flux[i][j] = flux[i][j] - value
                flux[j][i] = flux[j][i] + value
            for i in range(4):
                nx[i, p + 1, here, :] = flux[i][0]
                ny[i, p, mid, :] = flux[i][1]
            comb[p, here, :] = merge([flux[i][2] for i in range(4)])
            near = jnp.take_along_axis(table, bin_v[p, here, :], axis=1)
            for j in range(4):
                value = bars[j]
                if j < 3:
                    for i in range(4):
                        value = value - scaled[i] * diff[i][j]
                else:
                    value = value + scaled[3] * ((2.0 * coef_prod) * omega + cell[3] * near)
                value = value + (
                    pltpu.roll(jnp.where(low, 0.0, flux[j][2]), LANES - 1, 1)
                    - pltpu.roll(jnp.where(high, 0.0, flux[j][2]), 1, 1)
                )
                res[j, p, here, :] = value
        return carry

    plane(0, 0)
    plane(cx - 1, 0)
    start(second, 0)
    lax.fori_loop(1, cx - 1, plane, 0)
    start(second, 1)
    pack(w_send)
    start(second, 2)

    for i in range(4):
        ny[i, :, PAD - 1, :] = jnp.zeros((cx, LANES), f32)
        ny[i, :, PAD + cy, :] = jnp.zeros((cx, LANES), f32)

    def finish(p, carry):
        for t in range(tiles):
            lo = 8 * t
            here = slice(lo, lo + 8)
            up = slice(PAD + lo + 1, PAD + lo + 9)
            down = slice(PAD + lo - 1, PAD + lo + 7)
            for i in range(4):
                res[i, p, here, :] = res[i, p, here, :] + (
                    (nx[i, p + 2, here, :] - nx[i, p, here, :])
                    + (ny[i, p, up, :] - ny[i, p, down, :])
                )
        return carry

    lax.fori_loop(1, cx - 1, finish, 0)
    arrive(second, 0)
    finish(0, 0)
    finish(cx - 1, 0)
    arrive(second, 1)
    for i in range(4):
        res[i, :, 0, :] = res[i, :, 0, :] - y_halo[0, i]
        res[i, :, cy - 1, :] = res[i, :, cy - 1, :] + y_halo[1, i]
    arrive(second, 2)
    unpack(w_recv, -1.0)
    outer = jnp.logical_or(low, high)

    def sides(p, carry):
        for t in range(tiles):
            here = slice(8 * t, 8 * t + 8)
            edges = edge_t[p, here, :]
            for i in range(4):
                ends = pltpu.roll(edges, (LANES - 2 * i) % LANES, 1)
                ends = jnp.where(low, ends, pltpu.roll(edges, LANES - 2 - 2 * i, 1))
                res[i, p, here, :] = res[i, p, here, :] + jnp.where(outer, ends, 0.0)
        return carry

    lax.fori_loop(0, cx, sides, 0)
    stores = [
        pltpu.make_async_copy(res.at[0:3], ovel, store_sem.at[0]),
        pltpu.make_async_copy(res.at[3], onut, store_sem.at[1]),
    ]
    for copy in stores:
        copy.start()
    for d in range(3):
        sent(first, d)
        sent(second, d)
    for copy in stores:
        copy.wait()


def shards(counts, *args):
    velocity, nut_field = args[0], args[1]
    cx, cy, cz = nut_field.shape
    f32 = jnp.float32
    group = LANES // cy
    packed = (2, 4 * (cx // group), LANES)
    any_spec = pl.BlockSpec(memory_space=pl.ANY)
    return pl.pallas_call(
        functools.partial(section_kernel, counts),
        out_shape=(
            jax.ShapeDtypeStruct(velocity.shape, f32),
            jax.ShapeDtypeStruct(nut_field.shape, f32),
        ),
        in_specs=[any_spec] * 6 + [pl.BlockSpec(memory_space=pltpu.VMEM)],
        out_specs=(any_spec, any_spec),
        scratch_shapes=[
            pltpu.VMEM((4, cx + 2, cy + 2 * PAD, cz), f32),
            pltpu.VMEM((4, cx, cy, cz), f32),
            pltpu.VMEM((cx, cy, cz), jnp.int32),
            pltpu.VMEM((cx, cy, cz), jnp.int32),
            pltpu.VMEM((4, cx + 2, cy, cz), f32),
            pltpu.VMEM((4, cx, cy + 2 * PAD, cz), f32),
            pltpu.VMEM((4, cx, cy, cz), f32),
            pltpu.VMEM((cx, cy, cz), f32),
            pltpu.VMEM((cx, cy, cz), f32),
            pltpu.VMEM((2, 4, cx, cz), f32),
            pltpu.VMEM(packed, f32),
            pltpu.VMEM(packed, f32),
            pltpu.VMEM(packed, f32),
            pltpu.VMEM(packed, f32),
            pltpu.SemaphoreType.DMA((6,)),
            pltpu.SemaphoreType.DMA((2,)),
            pltpu.SemaphoreType.DMA((16,)),
            pltpu.SemaphoreType.DMA((16,)),
        ],
        compiler_params=pltpu.CompilerParams(
            collective_id=0, has_side_effects=True, vmem_limit_bytes=32 * 1024 * 1024
        ),
        name="section_adjoint",
    )(*args)


def solution(mesh):
    counts = tuple(mesh.shape[a] for a in AXES)
    field = P("gx", "gy", "gz")
    tensor = P(None, "gx", "gy", "gz")
    return jax.shard_map(
        functools.partial(shards, counts),
        mesh=mesh,
        in_specs=(tensor, field, tensor, field, field, field, P()),
        out_specs=(tensor, field),
        check_vma=False,
    )
```

```python
import functools

import jax
import jax.numpy as jnp
from jax import lax
from jax.experimental import pallas as pl
from jax.experimental.pallas import tpu as pltpu
from jax.sharding import PartitionSpec as P

des_length = 0.65
step_size = 0.25
kappa_sq = 0.1681
coef_prod = 0.1355
coef_dest = 3.239

MESH = pl.DeviceIdType.MESH
AXES = ("gx", "gy", "gz")
PAD = 8
LANES = 128


def section_kernel(
    counts, vel, nut, bvel, bnut, bins, mask, dist, ovel, onut,
    q, bar, bin_v, mask_v, dist_v, near, dz, nx, ny, parts, pick, place, y_halo,
    z_send, z_recv, w_send, w_recv, load_sem, send_sem, recv_sem,
):
    cx, cy = nut.shape[0], nut.shape[1]
    tiles = cy // 8
    group = LANES // cy
    groups = cx // group
    rows = pl.ds(PAD, cy)
    planes = pl.ds(1, cx)
    f32, bf16 = jnp.float32, jnp.bfloat16

    pos = [lax.axis_index(a) for a in AXES]
    has = [(pos[d] > 0, pos[d] < counts[d] - 1) for d in range(3)]
    peer = [({AXES[d]: pos[d] - 1}, {AXES[d]: pos[d] + 1}) for d in range(3)]

    loads = [
        pltpu.make_async_copy(vel, q.at[0:3, planes, rows, :], load_sem.at[0]),
        pltpu.make_async_copy(nut, q.at[3, planes, rows, :], load_sem.at[1]),
        pltpu.make_async_copy(bvel, bar.at[0:3], load_sem.at[2]),
        pltpu.make_async_copy(bnut, bar.at[3], load_sem.at[3]),
        pltpu.make_async_copy(mask, mask_v, load_sem.at[4]),
        pltpu.make_async_copy(bins, bin_v, load_sem.at[5]),
        pltpu.make_async_copy(dist, dist_v, load_sem.at[6]),
    ]
    for copy in loads:
        copy.start()

    barrier = pltpu.get_barrier_semaphore()
    for d in range(3):
        for s in range(2):
            @pl.when(has[d][s])
            def _():
                pl.semaphore_signal(barrier, inc=1, device_id=peer[d][s], device_id_type=MESH)

    def remote(src, dst, slot, d, s):
        return pltpu.make_async_remote_copy(
            src_ref=src, dst_ref=dst, send_sem=send_sem.at[slot], recv_sem=recv_sem.at[slot],
            device_id=peer[d][s], device_id_type=MESH,
        )

    first = [[None, None] for _ in range(3)]
    for s in range(2):
        end = (0, cx - 1)[s]
        halo = (cx + 1, 0)[s]
        first[0][s] = [
            remote(vel.at[:, end], q.at[0:3, halo, rows, :], 0 + s, 0, s),
            remote(nut.at[end], q.at[3, halo, rows, :], 2 + s, 0, s),
        ]
        end = (0, cy - 1)[s]
        halo = (PAD + cy, PAD - 1)[s]
        first[1][s] = [
            remote(vel.at[:, :, end, :], q.at[0:3, planes, halo, :], 4 + s, 1, s),
            remote(nut.at[:, end, :], q.at[3, planes, halo, :], 6 + s, 1, s),
        ]
        first[2][s] = [remote(z_send.at[s], z_recv.at[1 - s], 8 + s, 2, s)]
    second = [[None, None] for _ in range(3)]
    for s in range(2):
        end = (1, cx)[s]
        halo = (cx + 1, 0)[s]
        second[0][s] = [remote(nx.at[:, end], nx.at[:, halo], 10 + s, 0, s)]
        end = (PAD, PAD + cy - 1)[s]
        second[1][s] = [remote(ny.at[:, :, end, :], y_halo.at[1 - s], 12 + s, 1, s)]
        second[2][s] = [remote(w_send.at[s], w_recv.at[1 - s], 14 + s, 2, s)]

    def start(copies, d):
        for s in range(2):
            @pl.when(has[d][s])
            def _():
                for copy in copies[d][s]:
                    copy.start()

    def arrive(copies, d):
        for s in range(2):
            @pl.when(has[d][1 - s])
            def _():
                for copy in copies[d][s]:
                    copy.wait_recv()

    def sent(copies, d):
        for s in range(2):
            @pl.when(has[d][s])
            def _():
                for copy in copies[d][s]:
                    copy.wait_send()

    for s in range(2):
        @pl.when(jnp.logical_not(has[0][s]))
        def _():
            halo = (0, cx + 1)[s]
            q[:, halo, rows, :] = jnp.zeros((4, cy, LANES), f32)
            nx[:, halo] = jnp.zeros((4, cy, LANES), f32)

        @pl.when(jnp.logical_not(has[1][s]))
        def _():
            halo = (PAD - 1, PAD + cy)[s]
            for f in range(4):
                q[f, planes, halo, :] = jnp.zeros((cx, LANES), f32)
            y_halo[s] = jnp.zeros((4, cx, LANES), f32)

        @pl.when(jnp.logical_not(has[2][s]))
        def _():
            z_recv[s] = jnp.zeros((4 * groups, LANES), f32)
            w_recv[s] = jnp.zeros((4 * groups, LANES), f32)

    at = lax.broadcasted_iota(jnp.int32, (LANES, LANES), 0)
    to = lax.broadcasted_iota(jnp.int32, (LANES, LANES), 1)
    one = lambda where: jnp.where(where, 1.0, 0.0)
    change = (one(at == to + 1) - one(at == to - 1)).astype(bf16)
    for f in range(4):
        ends = one((at == LANES - 1) & (to == f)) + one((at == 0) & (to == 4 + f))
        for half_of in range(2):
            block = pl.ds(half_of * LANES, LANES)
            pick[f, block, 0:LANES] = change
            pick[f, block, LANES:2 * LANES] = ends.astype(bf16)
    at = lax.broadcasted_iota(jnp.int32, (16, LANES), 0) % 8
    to = lax.broadcasted_iota(jnp.int32, (16, LANES), 1)
    for f in range(4):
        place[:, f * LANES:(f + 1) * LANES] = (
            one((at == 4 + f) & (to == LANES - 1)) - one((at == f) & (to == 0))
        ).astype(bf16)

    def split(value):
        coarse = value.astype(bf16)
        return coarse, (value - coarse.astype(f32)).astype(bf16)

    def set_parts(f, p, value):
        coarse, fine = split(value)
        here = pl.ds(pl.multiple_of(p * cy, cy), cy)
        parts[here, 2 * f * LANES:(2 * f + 1) * LANES] = coarse
        parts[here, (2 * f + 1) * LANES:(2 * f + 2) * LANES] = fine

    def along_z(g, take, dst):
        here = pl.ds(g * LANES, LANES)
        ends = None
        for f in range(4):
            out = jnp.dot(
                parts[here, 2 * f * LANES:(2 * f + 2) * LANES], pick[f],
                preferred_element_type=f32,
            )
            take(f, g, out[:, :LANES].reshape(group, cy, LANES))
            ends = out[:, LANES:] if ends is None else ends + out[:, LANES:]
        turned = ends.T
        dst[1, 4 * g:4 * g + 4, :] = turned[0:4]
        dst[0, 4 * g:4 * g + 4, :] = turned[4:8]

    def add_halo(g, src, take):
        value = jnp.concatenate([src[0, 4 * g:4 * g + 4, :], src[1, 4 * g:4 * g + 4, :]], axis=0)
        coarse = value.astype(bf16).astype(f32)
        both = jnp.concatenate([coarse, value - coarse], axis=0).T.astype(bf16)
        out = jnp.dot(both, place[...], preferred_element_type=f32)
        for f in range(4):
            take(f, g, out[:, f * LANES:(f + 1) * LANES].reshape(group, cy, LANES))

    def set_dz(f, g, value):
        dz[f, g * group:(g + 1) * group] = value

    def add_dz(f, g, value):
        dz[f, g * group:(g + 1) * group] += value

    def add_res(f, g, value):
        if f < 3:
            ovel[f, g * group:(g + 1) * group] += value
        else:
            onut[g * group:(g + 1) * group] += value

    loads[0].wait()
    loads[1].wait()

    def part_plane(p, carry):
        for f in range(4):
            set_parts(f, p, q[f, p + 1, rows, :])
        return carry

    lax.fori_loop(0, cx, part_plane, 0)
    for g in range(groups):
        along_z(g, set_dz, z_send)

    present = sum(h.astype(jnp.int32) for pair in has for h in pair)
    pl.semaphore_wait(barrier, present)
    start(first, 2)
    start(first, 0)
    start(first, 1)

    for copy in loads[2:]:
        copy.wait()
    table = 1.0 / jnp.minimum(dist_v[...], des_length)
    table = table * table * (2.0 * (2.0 * coef_prod / kappa_sq - 2.0 * coef_dest))
    table = jnp.broadcast_to(
        jnp.pad(table, (0, LANES - table.shape[0])).reshape(1, LANES), (8, LANES)
    )

    def look(p, carry):
        for t in range(tiles):
            here = slice(8 * t, 8 * t + 8)
            near[p, here, :] = jnp.take_along_axis(table, bin_v[p, here, :], axis=1)
        return carry

    lax.fori_loop(0, cx, look, 0)

    arrive(first, 2)
    for g in range(groups):
        add_halo(g, z_recv, add_dz)
    arrive(first, 0)
    arrive(first, 1)

    half = 0.5 * step_size

    def plane(p, carry):
        along = [[] for _ in range(4)]
        for t in range(tiles):
            lo = 8 * t
            mid = slice(PAD + lo, PAD + lo + 8)
            up = slice(PAD + lo + 1, PAD + lo + 9)
            down = slice(PAD + lo - 1, PAD + lo + 7)
            here = slice(lo, lo + 8)
            cell = [q[f, p + 1, mid, :] for f in range(4)]
            diff = [
                [
                    q[f, p + 2, mid, :] - q[f, p, mid, :],
                    q[f, p + 1, up, :] - q[f, p + 1, down, :],
                    dz[f, p, here, :],
                ]
                for f in range(4)
            ]
            wet = jnp.where(mask_v[p, here, :] != 0, half, 0.0)
            bars = [bar[i, p, here, :] for i in range(4)]
            scaled = [wet * b for b in bars]
            spin = {
                (0, 1): diff[0][1] - diff[1][0],
                (0, 2): diff[0][2] - diff[2][0],
                (1, 2): diff[1][2] - diff[2][1],
            }
            total = 1.0 + 0.25 * (
                spin[0, 1] * spin[0, 1] + spin[0, 2] * spin[0, 2] + spin[1, 2] * spin[1, 2]
            )
            inverse = lax.rsqrt(total)
            omega = total * inverse
            weight = scaled[3] * cell[3] * inverse * (0.5 * coef_prod)
            flux = [[scaled[i] * cell[j] for j in range(3)] for i in range(4)]
            for (i, j), value in spin.items():
                turn = weight * value
                flux[i][j] = flux[i][j] - turn
                flux[j][i] = flux[j][i] + turn
            for i in range(4):
                nx[i, p + 1, here, :] = flux[i][0]
                ny[i, p, mid, :] = flux[i][1]
                along[i].append(flux[i][2])
            for j in range(3):
                value = bars[j]
                for i in range(4):
                    value = value - scaled[i] * diff[i][j]
                ovel[j, p, here, :] = value
            onut[p, here, :] = bars[3] + scaled[3] * (
                (2.0 * coef_prod) * omega + cell[3] * near[p, here, :]
            )
        for i in range(4):
            set_parts(i, p, jnp.concatenate(along[i], axis=0))
        return carry

    plane(0, 0)
    plane(cx - 1, 0)
    start(second, 0)
    lax.fori_loop(1, cx - 1, plane, 0)
    start(second, 1)
    for g in range(groups):
        along_z(g, add_res, w_send)
    start(second, 2)

    for i in range(4):
        ny[i, :, PAD - 1, :] = jnp.zeros((cx, LANES), f32)
        ny[i, :, PAD + cy, :] = jnp.zeros((cx, LANES), f32)

    def finish(p, carry):
        for t in range(tiles):
            lo = 8 * t
            here = slice(lo, lo + 8)
            up = slice(PAD + lo + 1, PAD + lo + 9)
            down = slice(PAD + lo - 1, PAD + lo + 7)
            for i in range(4):
                value = (nx[i, p + 2, here, :] - nx[i, p, here, :]) + (
                    ny[i, p, up, :] - ny[i, p, down, :]
                )
                if i < 3:
                    ovel[i, p, here, :] += value
                else:
                    onut[p, here, :] += value
        return carry

    lax.fori_loop(1, cx - 1, finish, 0)
    arrive(second, 0)
    finish(0, 0)
    finish(cx - 1, 0)
    arrive(second, 1)
    for i in range(3):
        ovel[i, :, 0, :] -= y_halo[0, i]
        ovel[i, :, cy - 1, :] += y_halo[1, i]
    onut[:, 0, :] -= y_halo[0, 3]
    onut[:, cy - 1, :] += y_halo[1, 3]
    arrive(second, 2)
    for g in range(groups):
        add_halo(g, w_recv, add_res)
    for d in range(3):
        sent(first, d)
        sent(second, d)


def shards(counts, *args):
    velocity, nut_field = args[0], args[1]
    cx, cy, cz = nut_field.shape
    f32 = jnp.float32
    group = LANES // cy
    packed = (2, 4 * (cx // group), LANES)
    hbm = pl.BlockSpec(memory_space=pltpu.HBM)
    vmem = pl.BlockSpec(memory_space=pltpu.VMEM)
    return pl.pallas_call(
        functools.partial(section_kernel, counts),
        out_shape=(
            jax.ShapeDtypeStruct(velocity.shape, f32),
            jax.ShapeDtypeStruct(nut_field.shape, f32),
        ),
        in_specs=[hbm] * 7,
        out_specs=(vmem, vmem),
        scratch_shapes=[
            pltpu.VMEM((4, cx + 2, cy + 2 * PAD, cz), f32),
            pltpu.VMEM((4, cx, cy, cz), f32),
            pltpu.VMEM((cx, cy, cz), jnp.int32),
            pltpu.VMEM((cx, cy, cz), jnp.int32),
            pltpu.VMEM(args[6].shape, f32),
            pltpu.VMEM((cx, cy, cz), f32),
            pltpu.VMEM((4, cx, cy, cz), f32),
            pltpu.VMEM((4, cx + 2, cy, cz), f32),
            pltpu.VMEM((4, cx, cy + 2 * PAD, cz), f32),
            pltpu.VMEM((cx * cy, 8 * LANES), jnp.bfloat16),
            pltpu.VMEM((4, 2 * LANES, 2 * LANES), jnp.bfloat16),
            pltpu.VMEM((16, 4 * LANES), jnp.bfloat16),
            pltpu.VMEM((2, 4, cx, cz), f32),
            pltpu.VMEM(packed, f32),
            pltpu.VMEM(packed, f32),
            pltpu.VMEM(packed, f32),
            pltpu.VMEM(packed, f32),
            pltpu.SemaphoreType.DMA((7,)),
            pltpu.SemaphoreType.DMA((16,)),
            pltpu.SemaphoreType.DMA((16,)),
        ],
        compiler_params=pltpu.CompilerParams(
            collective_id=0, has_side_effects=True, vmem_limit_bytes=32 * 1024 * 1024
        ),
        name="section_adjoint",
    )(*[pltpu.with_memory_space_constraint(x, pltpu.HBM) for x in args])


def solution(mesh):
    counts = tuple(mesh.shape[a] for a in AXES)
    field = P("gx", "gy", "gz")
    tensor = P(None, "gx", "gy", "gz")
    return jax.shard_map(
        functools.partial(shards, counts),
        mesh=mesh,
        in_specs=(tensor, field, tensor, field, field, field, P()),
        out_specs=(tensor, field),
        check_vma=False,
    )
```

```python
import functools

import jax
import jax.numpy as jnp
from jax import lax
from jax.experimental import pallas as pl
from jax.experimental.pallas import tpu as pltpu
from jax.sharding import PartitionSpec as P

des_length = 0.65
step_size = 0.25
kappa_sq = 0.1681
coef_prod = 0.1355
coef_dest = 3.239

MESH = pl.DeviceIdType.MESH
AXES = ("gx", "gy", "gz")
GREET = (1, 0, 0)
PAD = 8
LANES = 128


def section_kernel(
    counts, vel, nut, bvel, bnut, bins, mask, dist, ovel, onut,
    q, bar, bin_v, mask_v, dist_v, near, dz, nx, ny, parts, pick, place, y_halo,
    x_halo, z_send, z_recv, w_send, w_recv, load_sem, send_sem, recv_sem, ready,
):
    cx, cy = nut.shape[0], nut.shape[1]
    tiles = cy // 8
    group = LANES // cy
    groups = cx // group
    rows = pl.ds(PAD, cy)
    planes = pl.ds(1, cx)
    f32, bf16 = jnp.float32, jnp.bfloat16

    pos = [lax.axis_index(a) for a in AXES]
    has = [(pos[d] > 0, pos[d] < counts[d] - 1) for d in range(3)]
    peer = [({AXES[d]: pos[d] - 1}, {AXES[d]: pos[d] + 1}) for d in range(3)]

    barrier = pltpu.get_barrier_semaphore()
    for d in range(3):
        @pl.when(has[d][1 - GREET[d]])
        def _():
            pl.semaphore_signal(
                barrier, inc=1, device_id=peer[d][1 - GREET[d]], device_id_type=MESH
            )

    loads = [
        pltpu.make_async_copy(vel, q.at[0:3, planes, rows, :], load_sem.at[0]),
        pltpu.make_async_copy(nut, q.at[3, planes, rows, :], load_sem.at[1]),
        pltpu.make_async_copy(bvel, bar.at[0:3], load_sem.at[2]),
        pltpu.make_async_copy(bnut, bar.at[3], load_sem.at[3]),
        pltpu.make_async_copy(mask, mask_v, load_sem.at[4]),
        pltpu.make_async_copy(bins, bin_v, load_sem.at[5]),
        pltpu.make_async_copy(dist, dist_v, load_sem.at[6]),
    ]
    for copy in loads:
        copy.start()

    def remote(src, dst, slot, d, s):
        return pltpu.make_async_remote_copy(
            src_ref=src, dst_ref=dst, send_sem=send_sem.at[slot], recv_sem=recv_sem.at[slot],
            device_id=peer[d][s], device_id_type=MESH,
        )

    first = [[None, None] for _ in range(3)]
    late = [[None, None]]
    plain = [[None, None]]
    for s in range(2):
        end = (0, cx - 1)[s]
        halo = (cx + 1, 0)[s]
        first[0][s] = [remote(vel.at[1:3, end], q.at[1:3, halo, rows, :], 0 + s, 0, s)]
        late[0][s] = [
            remote(vel.at[0, end], x_halo.at[1 - s, 0], 2 + s, 0, s),
            remote(nut.at[end], x_halo.at[1 - s, 1], 16 + s, 0, s),
        ]
        end = (0, cy - 1)[s]
        halo = (PAD + cy, PAD - 1)[s]
        first[1][s] = [
            remote(vel.at[:, :, end, :], q.at[0:3, planes, halo, :], 4 + s, 1, s),
            remote(nut.at[:, end, :], q.at[3, planes, halo, :], 6 + s, 1, s),
        ]
        first[2][s] = [remote(z_send.at[s], z_recv.at[1 - s], 8 + s, 2, s)]
    second = [[None, None] for _ in range(3)]
    for s in range(2):
        end = (1, cx)[s]
        halo = (cx + 1, 0)[s]
        plain[0][s] = [
            remote(nx.at[0, end], nx.at[0, halo], 18 + s, 0, s),
            remote(nx.at[3, end], nx.at[3, halo], 20 + s, 0, s),
        ]
        second[0][s] = [remote(nx.at[1:3, end], nx.at[1:3, halo], 10 + s, 0, s)]
        end = (PAD, PAD + cy - 1)[s]
        second[1][s] = [remote(ny.at[:, :, end, :], y_halo.at[1 - s], 12 + s, 1, s)]
        second[2][s] = [remote(w_send.at[s], w_recv.at[1 - s], 14 + s, 2, s)]

    def start(copies, d, s):
        @pl.when(has[d][s])
        def _():
            for copy in copies[d][s]:
                copy.start()

    def arrive(copies, d, side):
        @pl.when(has[d][side])
        def _():
            for copy in copies[d][1 - side]:
                copy.wait_recv()

    def sent(copies, d):
        for s in range(2):
            @pl.when(has[d][s])
            def _():
                for copy in copies[d][s]:
                    copy.wait_send()

    for f in (0, 3):
        for halo in (0, cx + 1):
            q[f, halo, rows, :] = jnp.zeros((cy, LANES), f32)
    for s in range(2):
        @pl.when(jnp.logical_not(has[0][s]))
        def _():
            halo = (0, cx + 1)[s]
            q[1:3, halo, rows, :] = jnp.zeros((2, cy, LANES), f32)
            x_halo[s] = jnp.zeros((2, cy, LANES), f32)
            nx[:, halo] = jnp.zeros((4, cy, LANES), f32)

        @pl.when(jnp.logical_not(has[1][s]))
        def _():
            halo = (PAD - 1, PAD + cy)[s]
            for f in range(4):
                q[f, planes, halo, :] = jnp.zeros((cx, LANES), f32)
            y_halo[s] = jnp.zeros((4, cx, LANES), f32)

        @pl.when(jnp.logical_not(has[2][s]))
        def _():
            w_recv[s] = jnp.zeros((4 * groups, LANES), f32)

    at = lax.broadcasted_iota(jnp.int32, (LANES, LANES), 0)
    to = lax.broadcasted_iota(jnp.int32, (LANES, LANES), 1)
    one = lambda where: jnp.where(where, 1.0, 0.0)
    change = (one(at == to + 1) - one(at == to - 1)).astype(bf16)
    for f in range(4):
        ends = one((at == LANES - 1) & (to == f)) + one((at == 0) & (to == 4 + f))
        for half_of in range(2):
            block = pl.ds(half_of * LANES, LANES)
            pick[f, block, 0:LANES] = change
            pick[f, block, LANES:2 * LANES] = ends.astype(bf16)
    at = lax.broadcasted_iota(jnp.int32, (16, LANES), 0) % 8
    to = lax.broadcasted_iota(jnp.int32, (16, LANES), 1)
    for f in range(4):
        place[:, f * LANES:(f + 1) * LANES] = (
            one((at == 4 + f) & (to == LANES - 1)) - one((at == f) & (to == 0))
        ).astype(bf16)

    def split(value):
        coarse = value.astype(bf16)
        return coarse, (value - coarse.astype(f32)).astype(bf16)

    def set_parts(f, p, value):
        coarse, fine = split(value)
        here = pl.ds(pl.multiple_of(p * cy, cy), cy)
        parts[here, 2 * f * LANES:(2 * f + 1) * LANES] = coarse
        parts[here, (2 * f + 1) * LANES:(2 * f + 2) * LANES] = fine

    def along_z(g, take, dst, sides):
        here = pl.ds(g * LANES, LANES)
        ends = None
        for f in range(4):
            part = parts[here, 2 * f * LANES:(2 * f + 2) * LANES]
            if take is None:
                out = jnp.dot(part, pick[f, :, LANES:], preferred_element_type=f32)
            else:
                out = jnp.dot(part, pick[f], preferred_element_type=f32)
                take(f, g, out[:, :LANES].reshape(group, cy, LANES))
                out = out[:, LANES:]
            ends = out if ends is None else ends + out
        turned = ends.T
        if 1 in sides:
            dst[1, 4 * g:4 * g + 4, :] = turned[0:4]
        if 0 in sides:
            dst[0, 4 * g:4 * g + 4, :] = turned[4:8]

    def add_halo(g, src, take, sides):
        value = jnp.concatenate(
            [
                src[s, 4 * g:4 * g + 4, :] if s in sides else jnp.zeros((4, LANES), f32)
                for s in range(2)
            ],
            axis=0,
        )
        coarse = value.astype(bf16).astype(f32)
        both = jnp.concatenate([coarse, value - coarse], axis=0).T.astype(bf16)
        out = jnp.dot(both, place[...], preferred_element_type=f32)
        for f in range(4):
            take(f, g, out[:, f * LANES:(f + 1) * LANES].reshape(group, cy, LANES))

    def set_dz(f, g, value):
        dz[f, g * group:(g + 1) * group] = value

    def add_dz(f, g, value):
        dz[f, g * group:(g + 1) * group] += value

    def add_res(f, g, value):
        if f < 3:
            ovel[f, g * group:(g + 1) * group] += value
        else:
            onut[g * group:(g + 1) * group] += value

    loads[0].wait()
    loads[1].wait()

    def part_plane(p, carry):
        for f in range(4):
            set_parts(f, p, q[f, p + 1, rows, :])
        return carry

    lax.fori_loop(0, cx, part_plane, 0)
    for g in range(groups):
        along_z(g, set_dz, z_send, (0, 1))

    present = sum(has[d][GREET[d]].astype(jnp.int32) for d in range(3))
    @pl.when(present > 0)
    def _():
        pl.semaphore_wait(barrier, present)

    for d in (2, 0, 1):
        @pl.when(has[d][GREET[d]])
        def _():
            pl.semaphore_signal(
                ready.at[d], inc=1, device_id=peer[d][GREET[d]], device_id_type=MESH
            )
    for d in (2, 0, 1):
        start(first, d, GREET[d])

    for copy in loads[2:5]:
        copy.wait()
    half = 0.5 * step_size
    for p in (0, cx - 1):
        wet = jnp.where(mask_v[p] != 0, half, 0.0)
        for i in (0, 3):
            nx[i, p + 1] = wet * bar[i, p] * q[0, p + 1, rows, :]
    start(plain, 0, GREET[0])
    start(late, 0, GREET[0])
    for copy in loads[5:]:
        copy.wait()
    table = 1.0 / jnp.minimum(dist_v[...], des_length)
    table = table * table * (2.0 * (2.0 * coef_prod / kappa_sq - 2.0 * coef_dest))
    table = jnp.broadcast_to(
        jnp.pad(table, (0, LANES - table.shape[0])).reshape(1, LANES), (8, LANES)
    )

    def look(p, carry):
        for t in range(tiles):
            here = slice(8 * t, 8 * t + 8)
            near[p, here, :] = jnp.take_along_axis(table, bin_v[p, here, :], axis=1)
        return carry

    lax.fori_loop(0, cx, look, 0)

    for d in (1, 0, 2):
        @pl.when(has[d][1 - GREET[d]])
        def _():
            pl.semaphore_wait(ready.at[d], 1)
        start(first, d, 1 - GREET[d])
        if d == 0:
            start(plain, 0, 1 - GREET[0])
            start(late, 0, 1 - GREET[0])

    for d in (1, 0):
        for side in range(2):
            arrive(first, d, side)

    def plane(p, carry, inner=True, brief=False):
        along = [[] for _ in range(4)]
        for t in range(tiles):
            lo = 8 * t
            mid = slice(PAD + lo, PAD + lo + 8)
            up = slice(PAD + lo + 1, PAD + lo + 9)
            down = slice(PAD + lo - 1, PAD + lo + 7)
            here = slice(lo, lo + 8)
            cell = [q[f, p + 1, mid, :] for f in range(4)]
            diff = [
                [
                    q[f, p + 2, mid, :] - q[f, p, mid, :],
                    q[f, p + 1, up, :] - q[f, p + 1, down, :],
                    dz[f, p, here, :],
                ]
                for f in range(4)
            ]
            wet = jnp.where(mask_v[p, here, :] != 0, half, 0.0)
            bars = [bar[i, p, here, :] for i in range(4)]
            scaled = [wet * b for b in bars]
            spin = {
                (0, 1): diff[0][1] - diff[1][0],
                (0, 2): diff[0][2] - diff[2][0],
                (1, 2): diff[1][2] - diff[2][1],
            }
            total = 1.0 + 0.25 * (
                spin[0, 1] * spin[0, 1] + spin[0, 2] * spin[0, 2] + spin[1, 2] * spin[1, 2]
            )
            inverse = lax.rsqrt(total)
            omega = total * inverse
            weight = scaled[3] * cell[3] * inverse * (0.5 * coef_prod)
            flux = [[scaled[i] * cell[j] for j in range(3)] for i in range(4)]
            for (i, j), value in spin.items():
                turn = weight * value
                flux[i][j] = flux[i][j] - turn
                flux[j][i] = flux[j][i] + turn
            if brief:
                for i in range(4):
                    along[i].append(flux[i][2])
                continue
            for i in range(4):
                if i in (1, 2) or inner:
                    nx[i, p + 1, here, :] = flux[i][0]
                ny[i, p, mid, :] = flux[i][1]
                along[i].append(flux[i][2])
            for j in range(3):
                value = bars[j]
                for i in range(4):
                    value = value - scaled[i] * diff[i][j]
                ovel[j, p, here, :] = value
            onut[p, here, :] = bars[3] + scaled[3] * (
                (2.0 * coef_prod) * omega + cell[3] * near[p, here, :]
            )
        for i in range(4):
            set_parts(i, p, jnp.concatenate(along[i], axis=0))
        return carry

    @pl.when(has[2][0])
    def _():
        arrive(first, 2, 0)
        for g in range(groups):
            add_halo(g, z_recv, add_dz, (0,))
        lax.fori_loop(0, cx, functools.partial(plane, brief=True), 0)
        for g in range(groups):
            along_z(g, None, w_send, (0,))
        start(second, 2, 0)

    @pl.when(has[2][1])
    def _():
        arrive(first, 2, 1)
        for g in range(groups):
            add_halo(g, z_recv, add_dz, (1,))

    plane(0, 0, False)
    plane(cx - 1, 0, False)
    for s in range(2):
        start(second, 0, s)
    lax.fori_loop(1, cx - 1, plane, 0)
    for s in range(2):
        start(second, 1, s)
    for g in range(groups):
        along_z(g, add_res, w_send, (1,))
    start(second, 2, 1)

    for i in range(4):
        ny[i, :, PAD - 1, :] = jnp.zeros((cx, LANES), f32)
        ny[i, :, PAD + cy, :] = jnp.zeros((cx, LANES), f32)

    def finish(p, carry):
        for t in range(tiles):
            lo = 8 * t
            here = slice(lo, lo + 8)
            up = slice(PAD + lo + 1, PAD + lo + 9)
            down = slice(PAD + lo - 1, PAD + lo + 7)
            for i in range(4):
                value = (nx[i, p + 2, here, :] - nx[i, p, here, :]) + (
                    ny[i, p, up, :] - ny[i, p, down, :]
                )
                if i < 3:
                    ovel[i, p, here, :] += value
                else:
                    onut[p, here, :] += value
        return carry

    lax.fori_loop(1, cx - 1, finish, 0)
    for side in range(2):
        arrive(late, 0, side)
        arrive(plain, 0, side)
        arrive(second, 1, side)
    for s in range(2):
        p = (0, cx - 1)[s]
        wet = jnp.where(mask_v[p] != 0, (half, -half)[s], 0.0)
        ovel[0, p] += wet * (bar[0, p] * x_halo[s, 0] + bar[3, p] * x_halo[s, 1])
    for i in range(3):
        ovel[i, :, 0, :] -= y_halo[0, i]
        ovel[i, :, cy - 1, :] += y_halo[1, i]
    onut[:, 0, :] -= y_halo[0, 3]
    onut[:, cy - 1, :] += y_halo[1, 3]
    for d in range(3):
        sent(first, d)
    sent(late, 0)
    sent(plain, 0)
    for side in range(2):
        arrive(second, 0, side)
    finish(0, 0)
    finish(cx - 1, 0)
    for side in range(2):
        arrive(second, 2, side)
    for g in range(groups):
        add_halo(g, w_recv, add_res, (0, 1))
    for d in range(3):
        sent(second, d)


def out_kernel(vel_in, nut_in, vel_out, nut_out, sem):
    copies = [
        pltpu.make_async_copy(vel_in, vel_out, sem.at[0]),
        pltpu.make_async_copy(nut_in, nut_out, sem.at[1]),
    ]
    for copy in copies:
        copy.start()
    for copy in copies:
        copy.wait()


def shards(counts, *args):
    velocity, nut_field = args[0], args[1]
    cx, cy, cz = nut_field.shape
    f32 = jnp.float32
    group = LANES // cy
    packed = (2, 4 * (cx // group), LANES)
    hbm = pl.BlockSpec(memory_space=pltpu.HBM)
    vmem = pl.BlockSpec(memory_space=pltpu.VMEM)
    result = pl.pallas_call(
        functools.partial(section_kernel, counts),
        out_shape=(
            jax.ShapeDtypeStruct(velocity.shape, f32),
            jax.ShapeDtypeStruct(nut_field.shape, f32),
        ),
        in_specs=[hbm] * 7,
        out_specs=(vmem, vmem),
        scratch_shapes=[
            pltpu.VMEM((4, cx + 2, cy + 2 * PAD, cz), f32),
            pltpu.VMEM((4, cx, cy, cz), f32),
            pltpu.VMEM((cx, cy, cz), jnp.int32),
            pltpu.VMEM((cx, cy, cz), jnp.int32),
            pltpu.VMEM(args[6].shape, f32),
            pltpu.VMEM((cx, cy, cz), f32),
            pltpu.VMEM((4, cx, cy, cz), f32),
            pltpu.VMEM((4, cx + 2, cy, cz), f32),
            pltpu.VMEM((4, cx, cy + 2 * PAD, cz), f32),
            pltpu.VMEM((cx * cy, 8 * LANES), jnp.bfloat16),
            pltpu.VMEM((4, 2 * LANES, 2 * LANES), jnp.bfloat16),
            pltpu.VMEM((16, 4 * LANES), jnp.bfloat16),
            pltpu.VMEM((2, 4, cx, cz), f32),
            pltpu.VMEM((2, 2, cy, cz), f32),
            pltpu.VMEM(packed, f32),
            pltpu.VMEM(packed, f32),
            pltpu.VMEM(packed, f32),
            pltpu.VMEM(packed, f32),
            pltpu.SemaphoreType.DMA((7,)),
            pltpu.SemaphoreType.DMA((22,)),
            pltpu.SemaphoreType.DMA((22,)),
            pltpu.SemaphoreType.REGULAR((3,)),
        ],
        compiler_params=pltpu.CompilerParams(
            collective_id=0, has_side_effects=True, vmem_limit_bytes=32 * 1024 * 1024
        ),
        name="section_adjoint",
    )(*[pltpu.with_memory_space_constraint(x, pltpu.HBM) for x in args])
    return pl.pallas_call(
        out_kernel,
        out_shape=(
            jax.ShapeDtypeStruct(velocity.shape, f32),
            jax.ShapeDtypeStruct(nut_field.shape, f32),
        ),
        in_specs=[vmem] * 2,
        out_specs=(hbm, hbm),
        scratch_shapes=[pltpu.SemaphoreType.DMA((2,))],
        name="section_result",
    )(*[pltpu.with_memory_space_constraint(x, pltpu.VMEM) for x in result])


def solution(mesh):
    counts = tuple(mesh.shape[a] for a in AXES)
    field = P("gx", "gy", "gz")
    tensor = P(None, "gx", "gy", "gz")
    return jax.shard_map(
        functools.partial(shards, counts),
        mesh=mesh,
        in_specs=(tensor, field, tensor, field, field, field, P()),
        out_specs=(tensor, field),
        check_vma=False,
    )
```

```python
import functools

import jax
import jax.numpy as jnp
from jax import lax
from jax.experimental import pallas as pl
from jax.experimental.pallas import tpu as pltpu
from jax.sharding import PartitionSpec as P

des_length = 0.65
step_size = 0.25
kappa_sq = 0.1681
coef_prod = 0.1355
coef_dest = 3.239

MESH = pl.DeviceIdType.MESH
AXES = ("gx", "gy", "gz")
RUN = 4
PAD = 8
LANES = 128


def section_kernel(
    counts, vel, nut, bvel, bnut, bins, mask, dist, ovel, onut,
    q, bar, bin_v, mask_v, dist_v, near, dz, nx, ny, parts, pick, place, y_halo,
    x_halo, z_send, z_recv, w_recv, own, own_recv, cross, cross_recv,
    load_sem, send_sem, recv_sem, ready,
):
    cx, cy = nut.shape[0], nut.shape[1]
    tiles = cy // 8
    group = LANES // cy
    groups = cx // group
    rows = pl.ds(PAD, cy)
    planes = pl.ds(1, cx)
    f32, bf16 = jnp.float32, jnp.bfloat16

    pos = [lax.axis_index(a) for a in AXES]
    has = [(pos[d] > 0, pos[d] < counts[d] - 1) for d in range(3)]
    peer = [({AXES[d]: pos[d] - 1}, {AXES[d]: pos[d] + 1}) for d in range(3)]

    barrier = pltpu.get_barrier_semaphore()
    first_of_run = lax.rem(pos[0], RUN) == 0
    last_of_run = lax.rem(pos[0], RUN) == RUN - 1
    upper = 2 * pos[2] >= counts[2]
    upper_low = 2 * (pos[2] - 1) >= counts[2]
    not_ = jnp.logical_not
    greeted = [
        (has[0][0] & (not_(first_of_run) | upper), has[0][1] & (last_of_run | upper)),
        (has[1][0], has[1][1] & upper),
        (has[2][0], has[2][1] & upper),
    ]
    greets = [
        (has[0][0] & (first_of_run | upper), has[0][1] & (not_(last_of_run) | upper)),
        (has[1][0] & upper, has[1][1]),
        (has[2][0] & upper_low, has[2][1]),
    ]
    for d in range(3):
        for s in range(2):
            @pl.when(greets[d][s])
            def _():
                pl.semaphore_signal(barrier, inc=1, device_id=peer[d][s], device_id_type=MESH)

    loads = [
        pltpu.make_async_copy(vel, q.at[0:3, planes, rows, :], load_sem.at[0]),
        pltpu.make_async_copy(nut, q.at[3, planes, rows, :], load_sem.at[1]),
        pltpu.make_async_copy(bvel, bar.at[0:3], load_sem.at[2]),
        pltpu.make_async_copy(bnut, bar.at[3], load_sem.at[3]),
        pltpu.make_async_copy(mask, mask_v, load_sem.at[4]),
        pltpu.make_async_copy(bins, bin_v, load_sem.at[5]),
        pltpu.make_async_copy(dist, dist_v, load_sem.at[6]),
    ]
    for copy in loads:
        copy.start()

    def remote(src, dst, slot, d, s):
        return pltpu.make_async_remote_copy(
            src_ref=src, dst_ref=dst, send_sem=send_sem.at[slot], recv_sem=recv_sem.at[slot],
            device_id=peer[d][s], device_id_type=MESH,
        )

    first = [[None, None] for _ in range(3)]
    late = [[None, None]]
    plain = [[None, None]]
    for s in range(2):
        end = (0, cx - 1)[s]
        halo = (cx + 1, 0)[s]
        first[0][s] = [remote(vel.at[1:3, end], q.at[1:3, halo, rows, :], 0 + s, 0, s)]
        late[0][s] = [
            remote(vel.at[0, end], x_halo.at[1 - s, 0], 2 + s, 0, s),
            remote(nut.at[end], x_halo.at[1 - s, 1], 16 + s, 0, s),
        ]
        end = (0, cy - 1)[s]
        halo = (PAD + cy, PAD - 1)[s]
        first[1][s] = [
            remote(vel.at[:, :, end, :], q.at[0:3, planes, halo, :], 4 + s, 1, s),
            remote(nut.at[:, end, :], q.at[3, planes, halo, :], 6 + s, 1, s),
        ]
        first[2][s] = [remote(z_send.at[s], z_recv.at[1 - s], 8 + s, 2, s)]
    middle = [None, None, [None, None]]
    second = [[None, None] for _ in range(3)]
    for s in range(2):
        end = (1, cx)[s]
        halo = (cx + 1, 0)[s]
        plain[0][s] = [
            remote(nx.at[0, end], nx.at[0, halo], 18 + s, 0, s),
            remote(nx.at[3, end], nx.at[3, halo], 20 + s, 0, s),
        ]
        second[0][s] = [remote(nx.at[1:3, end], nx.at[1:3, halo], 10 + s, 0, s)]
        end = (PAD, PAD + cy - 1)[s]
        second[1][s] = [remote(ny.at[:, :, end, :], y_halo.at[1 - s], 12 + s, 1, s)]
        middle[2][s] = [remote(own.at[s], own_recv.at[1 - s], 22 + s, 2, s)]
        second[2][s] = [remote(cross.at[s], cross_recv.at[1 - s], 14 + s, 2, s)]

    def start(copies, d, s, where):
        @pl.when(where[d][s])
        def _():
            for copy in copies[d][s]:
                copy.start()

    def arrive(copies, d, side):
        @pl.when(has[d][side])
        def _():
            for copy in copies[d][1 - side]:
                copy.wait_recv()

    def sent(copies, d):
        for s in range(2):
            @pl.when(has[d][s])
            def _():
                for copy in copies[d][s]:
                    copy.wait_send()

    for f in (0, 3):
        for halo in (0, cx + 1):
            q[f, halo, rows, :] = jnp.zeros((cy, LANES), f32)
    for s in range(2):
        @pl.when(jnp.logical_not(has[0][s]))
        def _():
            halo = (0, cx + 1)[s]
            q[1:3, halo, rows, :] = jnp.zeros((2, cy, LANES), f32)
            x_halo[s] = jnp.zeros((2, cy, LANES), f32)
            nx[:, halo] = jnp.zeros((4, cy, LANES), f32)

        @pl.when(jnp.logical_not(has[1][s]))
        def _():
            halo = (PAD - 1, PAD + cy)[s]
            for f in range(4):
                q[f, planes, halo, :] = jnp.zeros((cx, LANES), f32)
            y_halo[s] = jnp.zeros((4, cx, LANES), f32)

        @pl.when(jnp.logical_not(has[2][s]))
        def _():
            w_recv[s] = jnp.zeros((4 * groups, LANES), f32)

    at = lax.broadcasted_iota(jnp.int32, (LANES, LANES), 0)
    to = lax.broadcasted_iota(jnp.int32, (LANES, LANES), 1)
    one = lambda where: jnp.where(where, 1.0, 0.0)
    change = (one(at == to + 1) - one(at == to - 1)).astype(bf16)
    for f in range(4):
        ends = one((at == LANES - 1) & (to == f)) + one((at == 0) & (to == 4 + f))
        for half_of in range(2):
            block = pl.ds(half_of * LANES, LANES)
            pick[f, block, 0:LANES] = change
            pick[f, block, LANES:2 * LANES] = ends.astype(bf16)
    at = lax.broadcasted_iota(jnp.int32, (16, LANES), 0) % 8
    to = lax.broadcasted_iota(jnp.int32, (16, LANES), 1)
    for f in range(4):
        place[:, f * LANES:(f + 1) * LANES] = (
            one((at == 4 + f) & (to == LANES - 1)) - one((at == f) & (to == 0))
        ).astype(bf16)

    def split(value):
        coarse = value.astype(bf16)
        return coarse, (value - coarse.astype(f32)).astype(bf16)

    def set_parts(f, p, value):
        coarse, fine = split(value)
        here = pl.ds(pl.multiple_of(p * cy, cy), cy)
        parts[here, 2 * f * LANES:(2 * f + 1) * LANES] = coarse
        parts[here, (2 * f + 1) * LANES:(2 * f + 2) * LANES] = fine

    def along_z(g, take, dst, sides, count=4, base=0):
        here = pl.ds(g * LANES, LANES)
        ends = None
        for f in range(count):
            part = parts[here, 2 * f * LANES:(2 * f + 2) * LANES]
            if take is None:
                out = jnp.dot(part, pick[f, :, LANES:], preferred_element_type=f32)
            elif not sides:
                out = jnp.dot(part, pick[f, :, :LANES], preferred_element_type=f32)
                take(f, g, out.reshape(group, cy, LANES))
                continue
            else:
                out = jnp.dot(part, pick[f], preferred_element_type=f32)
                take(f, g, out[:, :LANES].reshape(group, cy, LANES))
                out = out[:, LANES:]
            ends = out if ends is None else ends + out
        if not sides:
            return
        turned = ends.T
        at_row = base + 4 * g
        for s in sides:
            dst[s, at_row:at_row + 4, :] = (turned[4:8], turned[0:4])[s]

    def add_halo(g, src, take, sides):
        value = jnp.concatenate(
            [
                src[s, 4 * g:4 * g + 4, :] if s in sides else jnp.zeros((4, LANES), f32)
                for s in range(2)
            ],
            axis=0,
        )
        coarse = value.astype(bf16).astype(f32)
        both = jnp.concatenate([coarse, value - coarse], axis=0).T.astype(bf16)
        out = jnp.dot(both, place[...], preferred_element_type=f32)
        for f in range(4):
            take(f, g, out[:, f * LANES:(f + 1) * LANES].reshape(group, cy, LANES))

    def set_dz(f, g, value):
        dz[f, g * group:(g + 1) * group] = value

    def add_dz(f, g, value):
        dz[f, g * group:(g + 1) * group] += value

    def add_res(f, g, value):
        if f < 3:
            ovel[f, g * group:(g + 1) * group] += value
        else:
            onut[g * group:(g + 1) * group] += value

    present = sum(g.astype(jnp.int32) for pair in greeted for g in pair)

    @pl.when(present > 0)
    def _():
        pl.semaphore_wait(barrier, present)

    for d in (2, 0, 1):
        for s in range(2):
            @pl.when(greeted[d][s] & not_(greets[d][s]))
            def _():
                pl.semaphore_signal(
                    ready.at[d, 1 - s], inc=1, device_id=peer[d][s], device_id_type=MESH
                )
    for s in range(2):
        start(first, 0, s, greeted)
    for s in range(2):
        start(first, 1, s, greeted)

    loads[0].wait()
    loads[1].wait()

    def part_plane(p, carry):
        for f in range(4):
            set_parts(f, p, q[f, p + 1, rows, :])
        return carry

    lax.fori_loop(0, cx, part_plane, 0)
    for g in range(groups):
        along_z(g, set_dz, z_send, (0, 1))

    for s in range(2):
        start(first, 2, s, greeted)

    def told(d, s, copies):
        @pl.when(has[d][s] & not_(greeted[d][s]))
        def _():
            pl.semaphore_wait(ready.at[d, s], 1)
            for copy in copies:
                copy.start()

    told(1, 1, first[1][1])
    for s in (1, 0):
        told(0, s, first[0][s])

    for copy in loads[2:5]:
        copy.wait()
    half = 0.5 * step_size
    for p in (0, cx - 1):
        wet = jnp.where(mask_v[p] != 0, half, 0.0)
        for i in (0, 3):
            nx[i, p + 1] = wet * bar[i, p] * q[0, p + 1, rows, :]
    for s in range(2):
        start(plain, 0, s, has)
        start(late, 0, s, has)
    for copy in loads[5:]:
        copy.wait()
    table = 1.0 / jnp.minimum(dist_v[...], des_length)
    table = table * table * (2.0 * (2.0 * coef_prod / kappa_sq - 2.0 * coef_dest))
    table = jnp.broadcast_to(
        jnp.pad(table, (0, LANES - table.shape[0])).reshape(1, LANES), (8, LANES)
    )

    def look(p, carry):
        for t in range(tiles):
            here = slice(8 * t, 8 * t + 8)
            near[p, here, :] = jnp.take_along_axis(table, bin_v[p, here, :], axis=1)
        return carry

    lax.fori_loop(0, cx, look, 0)

    def extract(value, count, dst, base=0):
        def body(p, carry):
            for f in range(count):
                set_parts(f, p, value(f, p))
            return carry

        lax.fori_loop(0, cx, body, 0)
        for g in range(groups):
            along_z(g, None, dst, (0, 1), count, base)

    def wet_bar(f, p):
        return jnp.where(mask_v[p] != 0, half, 0.0) * bar[f, p]

    def own_value(f, p):
        if f == 0:
            return wet_bar(3, p) * q[3, p + 1, rows, :] * (0.5 * coef_prod)
        return dz[f - 1, p]

    above, below = pl.ds(PAD + 1, cy), pl.ds(PAD - 1, cy)

    def cross_value(f, p):
        if f == 0:
            return q[2, p + 2, rows, :] - q[2, p, rows, :]
        if f == 1:
            return q[2, p + 1, above, :] - q[2, p + 1, below, :]
        return (q[0, p + 1, above, :] - q[0, p + 1, below, :]) - (
            q[1, p + 2, rows, :] - q[1, p, rows, :]
        )

    extract(lambda f, p: wet_bar(f, p) * q[2, p + 1, rows, :], 4, own)
    extract(own_value, 3, own, 4 * groups)
    for s in range(2):
        start(middle, 2, s, greeted)

    for d in (1, 0):
        for side in range(2):
            arrive(first, d, side)
    extract(cross_value, 3, cross)
    for s in range(2):
        start(second, 2, s, greeted)
    told(2, 1, first[2][1] + middle[2][1] + second[2][1])

    def z_flux(side):
        take = lambda ref, f, base=0: ref[side, pl.ds(base + f, groups, stride=4), :]
        sign = (1.0, -1.0)[side]
        more = 4 * groups
        spin_02, spin_12 = [
            take(own_recv, 1 + f, more) + sign * take(z_send, f) - take(cross_recv, f)
            for f in range(2)
        ]
        spin_01 = take(cross_recv, 2)
        total = 1.0 + 0.25 * (spin_01 * spin_01 + spin_02 * spin_02 + spin_12 * spin_12)
        weight = take(own_recv, 0, more) * lax.rsqrt(total)
        turns = (weight * spin_02, weight * spin_12, 0.0, 0.0)
        for f in range(4):
            w_recv[side, pl.ds(f, groups, stride=4), :] = take(own_recv, f) - turns[f]

    for side in range(2):
        @pl.when(has[2][side])
        def _():
            arrive(first, 2, side)
            for g in range(groups):
                add_halo(g, z_recv, add_dz, (side,))

    def plane(p, carry, inner=True):
        along = [[] for _ in range(4)]
        for t in range(tiles):
            lo = 8 * t
            mid = slice(PAD + lo, PAD + lo + 8)
            up = slice(PAD + lo + 1, PAD + lo + 9)
            down = slice(PAD + lo - 1, PAD + lo + 7)
            here = slice(lo, lo + 8)
            cell = [q[f, p + 1, mid, :] for f in range(4)]
            diff = [
                [
                    q[f, p + 2, mid, :] - q[f, p, mid, :],
                    q[f, p + 1, up, :] - q[f, p + 1, down, :],
                    dz[f, p, here, :],
                ]
                for f in range(4)
            ]
            wet = jnp.where(mask_v[p, here, :] != 0, half, 0.0)
            bars = [bar[i, p, here, :] for i in range(4)]
            scaled = [wet * b for b in bars]
            spin = {
                (0, 1): diff[0][1] - diff[1][0],
                (0, 2): diff[0][2] - diff[2][0],
                (1, 2): diff[1][2] - diff[2][1],
            }
            total = 1.0 + 0.25 * (
                spin[0, 1] * spin[0, 1] + spin[0, 2] * spin[0, 2] + spin[1, 2] * spin[1, 2]
            )
            inverse = lax.rsqrt(total)
            omega = total * inverse
            weight = scaled[3] * cell[3] * inverse * (0.5 * coef_prod)
            flux = [[scaled[i] * cell[j] for j in range(3)] for i in range(4)]
            for (i, j), value in spin.items():
                turn = weight * value
                flux[i][j] = flux[i][j] - turn
                flux[j][i] = flux[j][i] + turn
            for i in range(4):
                if i in (1, 2) or inner:
                    nx[i, p + 1, here, :] = flux[i][0]
                ny[i, p, mid, :] = flux[i][1]
                along[i].append(flux[i][2])
            for j in range(3):
                value = bars[j]
                for i in range(4):
                    value = value - scaled[i] * diff[i][j]
                ovel[j, p, here, :] = value
            onut[p, here, :] = bars[3] + scaled[3] * (
                (2.0 * coef_prod) * omega + cell[3] * near[p, here, :]
            )
        for i in range(4):
            set_parts(i, p, jnp.concatenate(along[i], axis=0))
        return carry

    plane(0, 0, False)
    plane(cx - 1, 0, False)
    for s in range(2):
        start(second, 0, s, has)
    lax.fori_loop(1, cx - 1, plane, 0)
    for s in range(2):
        start(second, 1, s, has)
    for g in range(groups):
        along_z(g, add_res, None, ())

    for i in range(4):
        ny[i, :, PAD - 1, :] = jnp.zeros((cx, LANES), f32)
        ny[i, :, PAD + cy, :] = jnp.zeros((cx, LANES), f32)

    def finish(p, carry):
        for t in range(tiles):
            lo = 8 * t
            here = slice(lo, lo + 8)
            up = slice(PAD + lo + 1, PAD + lo + 9)
            down = slice(PAD + lo - 1, PAD + lo + 7)
            for i in range(4):
                value = (nx[i, p + 2, here, :] - nx[i, p, here, :]) + (
                    ny[i, p, up, :] - ny[i, p, down, :]
                )
                if i < 3:
                    ovel[i, p, here, :] += value
                else:
                    onut[p, here, :] += value
        return carry

    lax.fori_loop(1, cx - 1, finish, 0)
    for side in range(2):
        arrive(late, 0, side)
        arrive(plain, 0, side)
        arrive(second, 1, side)
    for s in range(2):
        p = (0, cx - 1)[s]
        wet = jnp.where(mask_v[p] != 0, (half, -half)[s], 0.0)
        ovel[0, p] += wet * (bar[0, p] * x_halo[s, 0] + bar[3, p] * x_halo[s, 1])
    for i in range(3):
        ovel[i, :, 0, :] -= y_halo[0, i]
        ovel[i, :, cy - 1, :] += y_halo[1, i]
    onut[:, 0, :] -= y_halo[0, 3]
    onut[:, cy - 1, :] += y_halo[1, 3]
    for d in range(3):
        sent(first, d)
    sent(late, 0)
    sent(plain, 0)
    for side in range(2):
        arrive(second, 0, side)
    finish(0, 0)
    finish(cx - 1, 0)
    for side in range(2):
        @pl.when(has[2][side])
        def _():
            arrive(middle, 2, side)
            arrive(second, 2, side)
            z_flux(side)

    for g in range(groups):
        add_halo(g, w_recv, add_res, (0, 1))
    sent(middle, 2)
    for d in range(3):
        sent(second, d)


def out_kernel(vel_in, nut_in, vel_out, nut_out, sem):
    copies = [
        pltpu.make_async_copy(vel_in, vel_out, sem.at[0]),
        pltpu.make_async_copy(nut_in, nut_out, sem.at[1]),
    ]
    for copy in copies:
        copy.start()
    for copy in copies:
        copy.wait()


def shards(counts, *args):
    velocity, nut_field = args[0], args[1]
    cx, cy, cz = nut_field.shape
    f32 = jnp.float32
    group = LANES // cy
    packed = (2, 4 * (cx // group), LANES)
    hbm = pl.BlockSpec(memory_space=pltpu.HBM)
    vmem = pl.BlockSpec(memory_space=pltpu.VMEM)
    result = pl.pallas_call(
        functools.partial(section_kernel, counts),
        out_shape=(
            jax.ShapeDtypeStruct(velocity.shape, f32),
            jax.ShapeDtypeStruct(nut_field.shape, f32),
        ),
        in_specs=[hbm] * 7,
        out_specs=(vmem, vmem),
        scratch_shapes=[
            pltpu.VMEM((4, cx + 2, cy + 2 * PAD, cz), f32),
            pltpu.VMEM((4, cx, cy, cz), f32),
            pltpu.VMEM((cx, cy, cz), jnp.int32),
            pltpu.VMEM((cx, cy, cz), jnp.int32),
            pltpu.VMEM(args[6].shape, f32),
            pltpu.VMEM((cx, cy, cz), f32),
            pltpu.VMEM((4, cx, cy, cz), f32),
            pltpu.VMEM((4, cx + 2, cy, cz), f32),
            pltpu.VMEM((4, cx, cy + 2 * PAD, cz), f32),
            pltpu.VMEM((cx * cy, 8 * LANES), jnp.bfloat16),
            pltpu.VMEM((4, 2 * LANES, 2 * LANES), jnp.bfloat16),
            pltpu.VMEM((16, 4 * LANES), jnp.bfloat16),
            pltpu.VMEM((2, 4, cx, cz), f32),
            pltpu.VMEM((2, 2, cy, cz), f32),
            pltpu.VMEM(packed, f32),
            pltpu.VMEM(packed, f32),
            pltpu.VMEM(packed, f32),
            pltpu.VMEM((2, 2 * packed[1], LANES), f32),
            pltpu.VMEM((2, 2 * packed[1], LANES), f32),
            pltpu.VMEM(packed, f32),
            pltpu.VMEM(packed, f32),
            pltpu.SemaphoreType.DMA((7,)),
            pltpu.SemaphoreType.DMA((24,)),
            pltpu.SemaphoreType.DMA((24,)),
            pltpu.SemaphoreType.REGULAR((3, 2)),
        ],
        compiler_params=pltpu.CompilerParams(
            collective_id=0, has_side_effects=True, vmem_limit_bytes=32 * 1024 * 1024
        ),
        name="section_adjoint",
    )(*[pltpu.with_memory_space_constraint(x, pltpu.HBM) for x in args])
    return pl.pallas_call(
        out_kernel,
        out_shape=(
            jax.ShapeDtypeStruct(velocity.shape, f32),
            jax.ShapeDtypeStruct(nut_field.shape, f32),
        ),
        in_specs=[vmem] * 2,
        out_specs=(hbm, hbm),
        scratch_shapes=[pltpu.SemaphoreType.DMA((2,))],
        name="section_result",
    )(*[pltpu.with_memory_space_constraint(x, pltpu.VMEM) for x in result])


def solution(mesh):
    counts = tuple(mesh.shape[a] for a in AXES)
    field = P("gx", "gy", "gz")
    tensor = P(None, "gx", "gy", "gz")
    return jax.shard_map(
        functools.partial(shards, counts),
        mesh=mesh,
        in_specs=(tensor, field, tensor, field, field, field, P()),
        out_specs=(tensor, field),
        check_vma=False,
    )
```

```python
import functools

import jax
import jax.numpy as jnp
from jax import lax
from jax.experimental import pallas as pl
from jax.experimental.pallas import tpu as pltpu
from jax.sharding import PartitionSpec as P

des_length = 0.65
step_size = 0.25
kappa_sq = 0.1681
coef_prod = 0.1355
coef_dest = 3.239

MESH = pl.DeviceIdType.MESH
AXES = ("gx", "gy", "gz")
RUN = 4
PAD = 8
LANES = 128


def section_kernel(
    counts, vel, nut, bvel, bnut, bins, mask, dist, ovel, onut,
    q, bar, bin_v, mask_v, dist_v, near, dz, nx, ny, parts, pick, place, y_halo,
    x_halo, z_send, z_recv, w_recv, own, own_recv, cross, cross_recv,
    load_sem, send_sem, recv_sem, ready,
):
    cx, cy = nut.shape[0], nut.shape[1]
    tiles = cy // 8
    group = LANES // cy
    groups = cx // group
    rows = pl.ds(PAD, cy)
    planes = pl.ds(1, cx)
    f32, bf16 = jnp.float32, jnp.bfloat16

    pos = [lax.axis_index(a) for a in AXES]
    has = [(pos[d] > 0, pos[d] < counts[d] - 1) for d in range(3)]
    peer = [({AXES[d]: pos[d] - 1}, {AXES[d]: pos[d] + 1}) for d in range(3)]

    barrier = pltpu.get_barrier_semaphore()
    first_of_run = lax.rem(pos[0], RUN) == 0
    last_of_run = lax.rem(pos[0], RUN) == RUN - 1
    upper = 2 * pos[2] >= counts[2]
    upper_low = 2 * (pos[2] - 1) >= counts[2]
    not_ = jnp.logical_not
    greeted = [
        (has[0][0] & (not_(first_of_run) | upper), has[0][1] & (last_of_run | upper)),
        (has[1][0], has[1][1] & upper),
        (has[2][0], has[2][1] & upper),
    ]
    greets = [
        (has[0][0] & (first_of_run | upper), has[0][1] & (not_(last_of_run) | upper)),
        (has[1][0] & upper, has[1][1]),
        (has[2][0] & upper_low, has[2][1]),
    ]
    for d in range(3):
        for s in range(2):
            @pl.when(greets[d][s])
            def _():
                pl.semaphore_signal(barrier, inc=1, device_id=peer[d][s], device_id_type=MESH)

    loads = [
        pltpu.make_async_copy(vel, q.at[0:3, planes, rows, :], load_sem.at[0]),
        pltpu.make_async_copy(nut, q.at[3, planes, rows, :], load_sem.at[1]),
        pltpu.make_async_copy(bvel, bar.at[0:3], load_sem.at[2]),
        pltpu.make_async_copy(bnut, bar.at[3], load_sem.at[3]),
        pltpu.make_async_copy(mask, mask_v, load_sem.at[4]),
        pltpu.make_async_copy(bins, bin_v, load_sem.at[5]),
        pltpu.make_async_copy(dist, dist_v, load_sem.at[6]),
    ]
    for copy in loads[:2]:
        copy.start()

    def remote(src, dst, slot, d, s):
        return pltpu.make_async_remote_copy(
            src_ref=src, dst_ref=dst, send_sem=send_sem.at[slot], recv_sem=recv_sem.at[slot],
            device_id=peer[d][s], device_id_type=MESH,
        )

    first = [[None, None] for _ in range(3)]
    late = [[None, None]]
    plain = [[None, None]]
    for s in range(2):
        end = (0, cx - 1)[s]
        halo = (cx + 1, 0)[s]
        first[0][s] = [remote(vel.at[1:3, end], q.at[1:3, halo, rows, :], 0 + s, 0, s)]
        late[0][s] = [
            remote(vel.at[0, end], x_halo.at[1 - s, 0], 2 + s, 0, s),
            remote(nut.at[end], x_halo.at[1 - s, 1], 16 + s, 0, s),
        ]
        end = (0, cy - 1)[s]
        halo = (PAD + cy, PAD - 1)[s]
        first[1][s] = [
            remote(vel.at[:, :, end, :], q.at[0:3, planes, halo, :], 4 + s, 1, s),
            remote(nut.at[:, end, :], q.at[3, planes, halo, :], 6 + s, 1, s),
        ]
        first[2][s] = [remote(z_send.at[s], z_recv.at[1 - s], 8 + s, 2, s)]
    middle = [None, None, [None, None]]
    second = [[None, None] for _ in range(3)]
    for s in range(2):
        end = (1, cx)[s]
        halo = (cx + 1, 0)[s]
        plain[0][s] = [
            remote(nx.at[0, end], nx.at[0, halo], 18 + s, 0, s),
            remote(nx.at[3, end], nx.at[3, halo], 20 + s, 0, s),
        ]
        second[0][s] = [remote(nx.at[1:3, end], nx.at[1:3, halo], 10 + s, 0, s)]
        end = (PAD, PAD + cy - 1)[s]
        second[1][s] = [remote(ny.at[:, :, end, :], y_halo.at[1 - s], 12 + s, 1, s)]
        middle[2][s] = [remote(own.at[s], own_recv.at[1 - s], 22 + s, 2, s)]
        second[2][s] = [remote(cross.at[s], cross_recv.at[1 - s], 14 + s, 2, s)]

    def start(copies, d, s, where):
        @pl.when(where[d][s])
        def _():
            for copy in copies[d][s]:
                copy.start()

    def arrive(copies, d, side):
        @pl.when(has[d][side])
        def _():
            for copy in copies[d][1 - side]:
                copy.wait_recv()

    def sent(copies, d):
        for s in range(2):
            @pl.when(has[d][s])
            def _():
                for copy in copies[d][s]:
                    copy.wait_send()

    for f in (0, 3):
        for halo in (0, cx + 1):
            q[f, halo, rows, :] = jnp.zeros((cy, LANES), f32)
    for s in range(2):
        @pl.when(jnp.logical_not(has[0][s]))
        def _():
            halo = (0, cx + 1)[s]
            q[1:3, halo, rows, :] = jnp.zeros((2, cy, LANES), f32)
            x_halo[s] = jnp.zeros((2, cy, LANES), f32)
            nx[:, halo] = jnp.zeros((4, cy, LANES), f32)

        @pl.when(jnp.logical_not(has[1][s]))
        def _():
            halo = (PAD - 1, PAD + cy)[s]
            for f in range(4):
                q[f, planes, halo, :] = jnp.zeros((cx, LANES), f32)
            y_halo[s] = jnp.zeros((4, cx, LANES), f32)

        @pl.when(jnp.logical_not(has[2][s]))
        def _():
            w_recv[s] = jnp.zeros((4 * groups, LANES), f32)

    at = lax.broadcasted_iota(jnp.int32, (LANES, LANES), 0)
    to = lax.broadcasted_iota(jnp.int32, (LANES, LANES), 1)
    one = lambda where: jnp.where(where, 1.0, 0.0)
    change = (one(at == to + 1) - one(at == to - 1)).astype(bf16)
    for f in range(4):
        ends = one((at == LANES - 1) & (to == f)) + one((at == 0) & (to == 4 + f))
        for half_of in range(2):
            block = pl.ds(half_of * LANES, LANES)
            pick[f, block, 0:LANES] = change
            pick[f, block, LANES:2 * LANES] = ends.astype(bf16)
    at = lax.broadcasted_iota(jnp.int32, (16, LANES), 0) % 8
    to = lax.broadcasted_iota(jnp.int32, (16, LANES), 1)
    for f in range(4):
        place[:, f * LANES:(f + 1) * LANES] = (
            one((at == 4 + f) & (to == LANES - 1)) - one((at == f) & (to == 0))
        ).astype(bf16)

    def split(value):
        coarse = value.astype(bf16)
        return coarse, (value - coarse.astype(f32)).astype(bf16)

    def set_parts(f, p, value):
        coarse, fine = split(value)
        here = pl.ds(pl.multiple_of(p * cy, cy), cy)
        parts[here, 2 * f * LANES:(2 * f + 1) * LANES] = coarse
        parts[here, (2 * f + 1) * LANES:(2 * f + 2) * LANES] = fine

    def along_z(g, take, dst, sides, count=4, base=0):
        here = pl.ds(g * LANES, LANES)
        ends = None
        for f in range(count):
            part = parts[here, 2 * f * LANES:(2 * f + 2) * LANES]
            if take is None:
                out = jnp.dot(part, pick[f, :, LANES:], preferred_element_type=f32)
            elif not sides:
                out = jnp.dot(part, pick[f, :, :LANES], preferred_element_type=f32)
                take(f, g, out.reshape(group, cy, LANES))
                continue
            else:
                out = jnp.dot(part, pick[f], preferred_element_type=f32)
                take(f, g, out[:, :LANES].reshape(group, cy, LANES))
                out = out[:, LANES:]
            ends = out if ends is None else ends + out
        if not sides:
            return
        turned = ends.T
        at_row = base + 4 * g
        for s in sides:
            dst[s, at_row:at_row + 4, :] = (turned[4:8], turned[0:4])[s]

    def add_halo(g, src, take, sides):
        value = jnp.concatenate(
            [
                src[s, 4 * g:4 * g + 4, :] if s in sides else jnp.zeros((4, LANES), f32)
                for s in range(2)
            ],
            axis=0,
        )
        coarse = value.astype(bf16).astype(f32)
        both = jnp.concatenate([coarse, value - coarse], axis=0).T.astype(bf16)
        out = jnp.dot(both, place[...], preferred_element_type=f32)
        for f in range(4):
            take(f, g, out[:, f * LANES:(f + 1) * LANES].reshape(group, cy, LANES))

    def set_dz(f, g, value):
        dz[f, g * group:(g + 1) * group] = value

    def add_dz(f, g, value):
        dz[f, g * group:(g + 1) * group] += value

    def add_res(f, g, value):
        if f < 3:
            ovel[f, g * group:(g + 1) * group] += value
        else:
            onut[g * group:(g + 1) * group] += value

    present = sum(g.astype(jnp.int32) for pair in greeted for g in pair)

    @pl.when(present > 0)
    def _():
        pl.semaphore_wait(barrier, present)

    for d in (2, 0, 1):
        for s in range(2):
            @pl.when(greeted[d][s] & not_(greets[d][s]))
            def _():
                pl.semaphore_signal(
                    ready.at[d, 1 - s], inc=1, device_id=peer[d][s], device_id_type=MESH
                )
    for s in range(2):
        start(first, 0, s, greeted)
    for s in range(2):
        start(first, 1, s, greeted)

    loads[0].wait()
    loads[1].wait()
    for copy in loads[2:]:
        copy.start()

    def part_plane(p, carry):
        for f in range(4):
            set_parts(f, p, q[f, p + 1, rows, :])
        return carry

    lax.fori_loop(0, cx, part_plane, 0)
    for g in range(groups):
        along_z(g, None, z_send, (0, 1))

    for s in range(2):
        start(first, 2, s, greeted)

    def told(d, s, copies):
        @pl.when(has[d][s] & not_(greeted[d][s]))
        def _():
            pl.semaphore_wait(ready.at[d, s], 1)
            for copy in copies:
                copy.start()

    told(1, 1, first[1][1])
    for s in (1, 0):
        told(0, s, first[0][s])

    for g in range(groups):
        along_z(g, set_dz, None, ())

    for copy in loads[2:5]:
        copy.wait()
    half = 0.5 * step_size
    for p in (0, cx - 1):
        wet = jnp.where(mask_v[p] != 0, half, 0.0)
        for i in (0, 3):
            nx[i, p + 1] = wet * bar[i, p] * q[0, p + 1, rows, :]
    for s in range(2):
        start(plain, 0, s, has)
        start(late, 0, s, has)
    for copy in loads[5:]:
        copy.wait()
    table = 1.0 / jnp.minimum(dist_v[...], des_length)
    table = table * table * (2.0 * (2.0 * coef_prod / kappa_sq - 2.0 * coef_dest))
    table = jnp.broadcast_to(
        jnp.pad(table, (0, LANES - table.shape[0])).reshape(1, LANES), (8, LANES)
    )

    def look(p, carry):
        for t in range(tiles):
            here = slice(8 * t, 8 * t + 8)
            near[p, here, :] = jnp.take_along_axis(table, bin_v[p, here, :], axis=1)
        return carry

    lax.fori_loop(0, cx, look, 0)

    def extract(value, count, dst, base=0):
        def body(p, carry):
            for f in range(count):
                set_parts(f, p, value(f, p))
            return carry

        lax.fori_loop(0, cx, body, 0)
        for g in range(groups):
            along_z(g, None, dst, (0, 1), count, base)

    def wet_bar(f, p):
        return jnp.where(mask_v[p] != 0, half, 0.0) * bar[f, p]

    def own_value(f, p):
        if f == 0:
            return wet_bar(3, p) * q[3, p + 1, rows, :] * (0.5 * coef_prod)
        return dz[f - 1, p]

    above, below = pl.ds(PAD + 1, cy), pl.ds(PAD - 1, cy)

    def cross_value(f, p):
        if f == 0:
            return q[2, p + 2, rows, :] - q[2, p, rows, :]
        if f == 1:
            return q[2, p + 1, above, :] - q[2, p + 1, below, :]
        return (q[0, p + 1, above, :] - q[0, p + 1, below, :]) - (
            q[1, p + 2, rows, :] - q[1, p, rows, :]
        )

    extract(lambda f, p: wet_bar(f, p) * q[2, p + 1, rows, :], 4, own)
    extract(own_value, 3, own, 4 * groups)
    for s in range(2):
        start(middle, 2, s, greeted)

    for d in (1, 0):
        for side in range(2):
            arrive(first, d, side)
    extract(cross_value, 3, cross)
    for s in range(2):
        start(second, 2, s, greeted)
    told(2, 1, first[2][1] + middle[2][1] + second[2][1])

    def z_flux(side):
        take = lambda ref, f, base=0: ref[side, pl.ds(base + f, groups, stride=4), :]
        sign = (1.0, -1.0)[side]
        more = 4 * groups
        spin_02, spin_12 = [
            take(own_recv, 1 + f, more) + sign * take(z_send, f) - take(cross_recv, f)
            for f in range(2)
        ]
        spin_01 = take(cross_recv, 2)
        total = 1.0 + 0.25 * (spin_01 * spin_01 + spin_02 * spin_02 + spin_12 * spin_12)
        weight = take(own_recv, 0, more) * lax.rsqrt(total)
        turns = (weight * spin_02, weight * spin_12, 0.0, 0.0)
        for f in range(4):
            w_recv[side, pl.ds(f, groups, stride=4), :] = take(own_recv, f) - turns[f]

    for side in range(2):
        @pl.when(has[2][side])
        def _():
            arrive(first, 2, side)
            for g in (0, groups - 1):
                add_halo(g, z_recv, add_dz, (side,))

    def plane(p, carry, inner=True):
        along = [[] for _ in range(4)]
        for t in range(tiles):
            lo = 8 * t
            mid = slice(PAD + lo, PAD + lo + 8)
            up = slice(PAD + lo + 1, PAD + lo + 9)
            down = slice(PAD + lo - 1, PAD + lo + 7)
            here = slice(lo, lo + 8)
            cell = [q[f, p + 1, mid, :] for f in range(4)]
            diff = [
                [
                    q[f, p + 2, mid, :] - q[f, p, mid, :],
                    q[f, p + 1, up, :] - q[f, p + 1, down, :],
                    dz[f, p, here, :],
                ]
                for f in range(4)
            ]
            wet = jnp.where(mask_v[p, here, :] != 0, half, 0.0)
            bars = [bar[i, p, here, :] for i in range(4)]
            scaled = [wet * b for b in bars]
            spin = {
                (0, 1): diff[0][1] - diff[1][0],
                (0, 2): diff[0][2] - diff[2][0],
                (1, 2): diff[1][2] - diff[2][1],
            }
            total = 1.0 + 0.25 * (
                spin[0, 1] * spin[0, 1] + spin[0, 2] * spin[0, 2] + spin[1, 2] * spin[1, 2]
            )
            inverse = lax.rsqrt(total)
            omega = total * inverse
            weight = scaled[3] * cell[3] * inverse * (0.5 * coef_prod)
            flux = [[scaled[i] * cell[j] for j in range(3)] for i in range(4)]
            for (i, j), value in spin.items():
                turn = weight * value
                flux[i][j] = flux[i][j] - turn
                flux[j][i] = flux[j][i] + turn
            for i in range(4):
                if i in (1, 2) or inner:
                    nx[i, p + 1, here, :] = flux[i][0]
                ny[i, p, mid, :] = flux[i][1]
                along[i].append(flux[i][2])
            for j in range(3):
                value = bars[j]
                for i in range(4):
                    value = value - scaled[i] * diff[i][j]
                ovel[j, p, here, :] = value
            onut[p, here, :] = bars[3] + scaled[3] * (
                (2.0 * coef_prod) * omega + cell[3] * near[p, here, :]
            )
        for i in range(4):
            set_parts(i, p, jnp.concatenate(along[i], axis=0))
        return carry

    plane(0, 0, False)
    plane(cx - 1, 0, False)
    for s in range(2):
        start(second, 0, s, has)
    for side in range(2):
        @pl.when(has[2][side])
        def _():
            for g in range(1, groups - 1):
                add_halo(g, z_recv, add_dz, (side,))

    lax.fori_loop(1, cx - 1, plane, 0)
    for s in range(2):
        start(second, 1, s, has)
    for g in range(groups):
        along_z(g, add_res, None, ())

    for i in range(4):
        ny[i, :, PAD - 1, :] = jnp.zeros((cx, LANES), f32)
        ny[i, :, PAD + cy, :] = jnp.zeros((cx, LANES), f32)

    def finish(p, carry):
        for t in range(tiles):
            lo = 8 * t
            here = slice(lo, lo + 8)
            up = slice(PAD + lo + 1, PAD + lo + 9)
            down = slice(PAD + lo - 1, PAD + lo + 7)
            for i in range(4):
                value = (nx[i, p + 2, here, :] - nx[i, p, here, :]) + (
                    ny[i, p, up, :] - ny[i, p, down, :]
                )
                if i < 3:
                    ovel[i, p, here, :] += value
                else:
                    onut[p, here, :] += value
        return carry

    lax.fori_loop(1, cx - 1, finish, 0)
    for side in range(2):
        arrive(late, 0, side)
        arrive(plain, 0, side)
        arrive(second, 1, side)
    for s in range(2):
        p = (0, cx - 1)[s]
        wet = jnp.where(mask_v[p] != 0, (half, -half)[s], 0.0)
        ovel[0, p] += wet * (bar[0, p] * x_halo[s, 0] + bar[3, p] * x_halo[s, 1])
    for i in range(3):
        ovel[i, :, 0, :] -= y_halo[0, i]
        ovel[i, :, cy - 1, :] += y_halo[1, i]
    onut[:, 0, :] -= y_halo[0, 3]
    onut[:, cy - 1, :] += y_halo[1, 3]
    for d in range(3):
        sent(first, d)
        sent(second, d)
    sent(middle, 2)
    sent(late, 0)
    sent(plain, 0)
    def end_x():
        for side in range(2):
            arrive(second, 0, side)
        finish(0, 0)
        finish(cx - 1, 0)

    def end_z():
        for side in range(2):
            @pl.when(has[2][side])
            def _():
                arrive(middle, 2, side)
                arrive(second, 2, side)
                z_flux(side)

        for g in range(groups):
            add_halo(g, w_recv, add_res, (0, 1))

    @pl.when(first_of_run)
    def _():
        end_z()
        end_x()

    @pl.when(not_(first_of_run))
    def _():
        end_x()
        end_z()


def out_kernel(vel_in, nut_in, vel_out, nut_out, sem):
    copies = [
        pltpu.make_async_copy(vel_in, vel_out, sem.at[0]),
        pltpu.make_async_copy(nut_in, nut_out, sem.at[1]),
    ]
    for copy in copies:
        copy.start()
    for copy in copies:
        copy.wait()


def shards(counts, *args):
    velocity, nut_field = args[0], args[1]
    cx, cy, cz = nut_field.shape
    f32 = jnp.float32
    group = LANES // cy
    packed = (2, 4 * (cx // group), LANES)
    hbm = pl.BlockSpec(memory_space=pltpu.HBM)
    vmem = pl.BlockSpec(memory_space=pltpu.VMEM)
    result = pl.pallas_call(
        functools.partial(section_kernel, counts),
        out_shape=(
            jax.ShapeDtypeStruct(velocity.shape, f32),
            jax.ShapeDtypeStruct(nut_field.shape, f32),
        ),
        in_specs=[hbm] * 7,
        out_specs=(vmem, vmem),
        scratch_shapes=[
            pltpu.VMEM((4, cx + 2, cy + 2 * PAD, cz), f32),
            pltpu.VMEM((4, cx, cy, cz), f32),
            pltpu.VMEM((cx, cy, cz), jnp.int32),
            pltpu.VMEM((cx, cy, cz), jnp.int32),
            pltpu.VMEM(args[6].shape, f32),
            pltpu.VMEM((cx, cy, cz), f32),
            pltpu.VMEM((4, cx, cy, cz), f32),
            pltpu.VMEM((4, cx + 2, cy, cz), f32),
            pltpu.VMEM((4, cx, cy + 2 * PAD, cz), f32),
            pltpu.VMEM((cx * cy, 8 * LANES), jnp.bfloat16),
            pltpu.VMEM((4, 2 * LANES, 2 * LANES), jnp.bfloat16),
            pltpu.VMEM((16, 4 * LANES), jnp.bfloat16),
            pltpu.VMEM((2, 4, cx, cz), f32),
            pltpu.VMEM((2, 2, cy, cz), f32),
            pltpu.VMEM(packed, f32),
            pltpu.VMEM(packed, f32),
            pltpu.VMEM(packed, f32),
            pltpu.VMEM((2, 2 * packed[1], LANES), f32),
            pltpu.VMEM((2, 2 * packed[1], LANES), f32),
            pltpu.VMEM(packed, f32),
            pltpu.VMEM(packed, f32),
            pltpu.SemaphoreType.DMA((7,)),
            pltpu.SemaphoreType.DMA((24,)),
            pltpu.SemaphoreType.DMA((24,)),
            pltpu.SemaphoreType.REGULAR((3, 2)),
        ],
        compiler_params=pltpu.CompilerParams(
            collective_id=0, has_side_effects=True, vmem_limit_bytes=32 * 1024 * 1024
        ),
        name="section_adjoint",
    )(*[pltpu.with_memory_space_constraint(x, pltpu.HBM) for x in args])
    return pl.pallas_call(
        out_kernel,
        out_shape=(
            jax.ShapeDtypeStruct(velocity.shape, f32),
            jax.ShapeDtypeStruct(nut_field.shape, f32),
        ),
        in_specs=[vmem] * 2,
        out_specs=(hbm, hbm),
        scratch_shapes=[pltpu.SemaphoreType.DMA((2,))],
        name="section_result",
    )(*[pltpu.with_memory_space_constraint(x, pltpu.VMEM) for x in result])


def solution(mesh):
    counts = tuple(mesh.shape[a] for a in AXES)
    field = P("gx", "gy", "gz")
    tensor = P(None, "gx", "gy", "gz")
    return jax.shard_map(
        functools.partial(shards, counts),
        mesh=mesh,
        in_specs=(tensor, field, tensor, field, field, field, P()),
        out_specs=(tensor, field),
        check_vma=False,
    )
```

```python
import functools

import jax
import jax.numpy as jnp
from jax import lax
from jax.experimental import pallas as pl
from jax.experimental.pallas import tpu as pltpu
from jax.sharding import PartitionSpec as P

des_length = 0.65
step_size = 0.25
kappa_sq = 0.1681
coef_prod = 0.1355
coef_dest = 3.239

MESH = pl.DeviceIdType.MESH
AXES = ("gx", "gy", "gz")
RUN = 4
PAD = 8
LANES = 128


def section_kernel(
    counts, vel, nut, bvel, bnut, bins, mask, dist, ovel, onut,
    q, bar, bin_v, mask_v, dist_v, near, dz, nx, ny, parts, pick, place, y_halo,
    x_halo, z_send, z_recv, w_recv, own, own_recv, cross, cross_recv,
    load_sem, send_sem, recv_sem, ready,
):
    cx, cy = nut.shape[0], nut.shape[1]
    tiles = cy // 8
    group = LANES // cy
    groups = cx // group
    rows = pl.ds(PAD, cy)
    planes = pl.ds(1, cx)
    f32, bf16 = jnp.float32, jnp.bfloat16

    pos = [lax.axis_index(a) for a in AXES]
    has = [(pos[d] > 0, pos[d] < counts[d] - 1) for d in range(3)]
    peer = [({AXES[d]: pos[d] - 1}, {AXES[d]: pos[d] + 1}) for d in range(3)]

    barrier = pltpu.get_barrier_semaphore()
    first_of_run = lax.rem(pos[0], RUN) == 0
    last_of_run = lax.rem(pos[0], RUN) == RUN - 1
    upper = 2 * pos[2] >= counts[2]
    upper_low = 2 * (pos[2] - 1) >= counts[2]
    not_ = jnp.logical_not
    greeted = [
        (has[0][0] & (not_(first_of_run) | upper), has[0][1] & (last_of_run | upper)),
        (has[1][0], has[1][1] & upper),
        (has[2][0], has[2][1] & upper),
    ]
    greets = [
        (has[0][0] & (first_of_run | upper), has[0][1] & (not_(last_of_run) | upper)),
        (has[1][0] & upper, has[1][1]),
        (has[2][0] & upper_low, has[2][1]),
    ]
    for d in range(3):
        for s in range(2):
            @pl.when(greets[d][s])
            def _():
                pl.semaphore_signal(barrier, inc=1, device_id=peer[d][s], device_id_type=MESH)

    loads = [
        pltpu.make_async_copy(vel, q.at[0:3, planes, rows, :], load_sem.at[0]),
        pltpu.make_async_copy(nut, q.at[3, planes, rows, :], load_sem.at[1]),
        pltpu.make_async_copy(bvel, bar.at[0:3], load_sem.at[2]),
        pltpu.make_async_copy(bnut, bar.at[3], load_sem.at[3]),
        pltpu.make_async_copy(mask, mask_v, load_sem.at[4]),
        pltpu.make_async_copy(bins, bin_v, load_sem.at[5]),
        pltpu.make_async_copy(dist, dist_v, load_sem.at[6]),
    ]
    for copy in loads[:2]:
        copy.start()

    def remote(src, dst, slot, d, s):
        return pltpu.make_async_remote_copy(
            src_ref=src, dst_ref=dst, send_sem=send_sem.at[slot], recv_sem=recv_sem.at[slot],
            device_id=peer[d][s], device_id_type=MESH,
        )

    first = [[None, None] for _ in range(3)]
    late = [[None, None]]
    plain = [[None, None]]
    for s in range(2):
        end = (0, cx - 1)[s]
        halo = (cx + 1, 0)[s]
        first[0][s] = [remote(vel.at[1:3, end], q.at[1:3, halo, rows, :], 0 + s, 0, s)]
        late[0][s] = [
            remote(vel.at[0, end], x_halo.at[1 - s, 0], 2 + s, 0, s),
            remote(nut.at[end], x_halo.at[1 - s, 1], 16 + s, 0, s),
        ]
        end = (0, cy - 1)[s]
        halo = (PAD + cy, PAD - 1)[s]
        first[1][s] = [
            remote(vel.at[:, :, end, :], q.at[0:3, planes, halo, :], 4 + s, 1, s),
            remote(nut.at[:, end, :], q.at[3, planes, halo, :], 6 + s, 1, s),
        ]
        first[2][s] = [remote(z_send.at[s], z_recv.at[1 - s], 8 + s, 2, s)]
    middle = [None, None, [None, None]]
    second = [[None, None] for _ in range(3)]
    for s in range(2):
        end = (1, cx)[s]
        halo = (cx + 1, 0)[s]
        plain[0][s] = [
            remote(nx.at[0, end], nx.at[0, halo], 18 + s, 0, s),
            remote(nx.at[3, end], nx.at[3, halo], 20 + s, 0, s),
        ]
        second[0][s] = [remote(nx.at[1:3, end], nx.at[1:3, halo], 10 + s, 0, s)]
        end = (PAD, PAD + cy - 1)[s]
        second[1][s] = [remote(ny.at[:, :, end, :], y_halo.at[1 - s], 12 + s, 1, s)]
        middle[2][s] = [remote(own.at[s], own_recv.at[1 - s], 22 + s, 2, s)]
        second[2][s] = [remote(cross.at[s], cross_recv.at[1 - s], 14 + s, 2, s)]

    def start(copies, d, s, where):
        @pl.when(where[d][s])
        def _():
            for copy in copies[d][s]:
                copy.start()

    def arrive(copies, d, side):
        @pl.when(has[d][side])
        def _():
            for copy in copies[d][1 - side]:
                copy.wait_recv()

    def sent(copies, d):
        for s in range(2):
            @pl.when(has[d][s])
            def _():
                for copy in copies[d][s]:
                    copy.wait_send()

    for f in (0, 3):
        for halo in (0, cx + 1):
            q[f, halo, rows, :] = jnp.zeros((cy, LANES), f32)
    for s in range(2):
        @pl.when(jnp.logical_not(has[0][s]))
        def _():
            halo = (0, cx + 1)[s]
            q[1:3, halo, rows, :] = jnp.zeros((2, cy, LANES), f32)
            x_halo[s] = jnp.zeros((2, cy, LANES), f32)
            nx[:, halo] = jnp.zeros((4, cy, LANES), f32)

        @pl.when(jnp.logical_not(has[1][s]))
        def _():
            halo = (PAD - 1, PAD + cy)[s]
            for f in range(4):
                q[f, planes, halo, :] = jnp.zeros((cx, LANES), f32)
            y_halo[s] = jnp.zeros((4, cx, LANES), f32)

        @pl.when(jnp.logical_not(has[2][s]))
        def _():
            w_recv[s] = jnp.zeros((4 * groups, LANES), f32)

    at = lax.broadcasted_iota(jnp.int32, (LANES, LANES), 0)
    to = lax.broadcasted_iota(jnp.int32, (LANES, LANES), 1)
    one = lambda where: jnp.where(where, 1.0, 0.0)
    change = (one(at == to + 1) - one(at == to - 1)).astype(bf16)
    for f in range(4):
        ends = one((at == LANES - 1) & (to == f)) + one((at == 0) & (to == 4 + f))
        for half_of in range(2):
            block = pl.ds(half_of * LANES, LANES)
            pick[f, block, 0:LANES] = change
            pick[f, block, LANES:2 * LANES] = ends.astype(bf16)
    at = lax.broadcasted_iota(jnp.int32, (16, LANES), 0) % 8
    to = lax.broadcasted_iota(jnp.int32, (16, LANES), 1)
    for f in range(4):
        place[:, f * LANES:(f + 1) * LANES] = (
            one((at == 4 + f) & (to == LANES - 1)) - one((at == f) & (to == 0))
        ).astype(bf16)

    def split(value):
        coarse = value.astype(bf16)
        return coarse, (value - coarse.astype(f32)).astype(bf16)

    def set_parts(f, p, value):
        coarse, fine = split(value)
        here = pl.ds(pl.multiple_of(p * cy, cy), cy)
        parts[here, 2 * f * LANES:(2 * f + 1) * LANES] = coarse
        parts[here, (2 * f + 1) * LANES:(2 * f + 2) * LANES] = fine

    def along_z(g, take, dst, sides, count=4, base=0):
        here = pl.ds(g * LANES, LANES)
        ends = None
        for f in range(count):
            part = parts[here, 2 * f * LANES:(2 * f + 2) * LANES]
            if take is None:
                out = jnp.dot(part, pick[f, :, LANES:], preferred_element_type=f32)
            elif not sides:
                out = jnp.dot(part, pick[f, :, :LANES], preferred_element_type=f32)
                take(f, g, out.reshape(group, cy, LANES))
                continue
            else:
                out = jnp.dot(part, pick[f], preferred_element_type=f32)
                take(f, g, out[:, :LANES].reshape(group, cy, LANES))
                out = out[:, LANES:]
            ends = out if ends is None else ends + out
        if not sides:
            return
        turned = ends.T
        at_row = base + 4 * g
        for s in sides:
            dst[s, at_row:at_row + 4, :] = (turned[4:8], turned[0:4])[s]

    def add_halo(g, src, take, sides):
        value = jnp.concatenate(
            [
                src[s, 4 * g:4 * g + 4, :] if s in sides else jnp.zeros((4, LANES), f32)
                for s in range(2)
            ],
            axis=0,
        )
        coarse = value.astype(bf16).astype(f32)
        both = jnp.concatenate([coarse, value - coarse], axis=0).T.astype(bf16)
        out = jnp.dot(both, place[...], preferred_element_type=f32)
        for f in range(4):
            take(f, g, out[:, f * LANES:(f + 1) * LANES].reshape(group, cy, LANES))

    def set_dz(f, g, value):
        dz[f, g * group:(g + 1) * group] = value

    def add_dz(f, g, value):
        dz[f, g * group:(g + 1) * group] += value

    def add_res(f, g, value):
        if f < 3:
            ovel[f, g * group:(g + 1) * group] += value
        else:
            onut[g * group:(g + 1) * group] += value

    present = sum(g.astype(jnp.int32) for pair in greeted for g in pair)

    @pl.when(present > 0)
    def _():
        pl.semaphore_wait(barrier, present)

    for d in (2, 0, 1):
        for s in range(2):
            @pl.when(greeted[d][s] & not_(greets[d][s]))
            def _():
                pl.semaphore_signal(
                    ready.at[d, 1 - s], inc=1, device_id=peer[d][s], device_id_type=MESH
                )
    for s in range(2):
        start(first, 0, s, greeted)
    for s in range(2):
        start(first, 1, s, greeted)

    loads[0].wait()
    loads[1].wait()
    for copy in loads[2:]:
        copy.start()

    def part_plane(p, carry):
        for f in range(4):
            set_parts(f, p, q[f, p + 1, rows, :])
        return carry

    lax.fori_loop(0, cx, part_plane, 0, unroll=4)
    for g in range(groups):
        along_z(g, None, z_send, (0, 1))

    for s in range(2):
        start(first, 2, s, greeted)

    def told(d, s, copies):
        @pl.when(has[d][s] & not_(greeted[d][s]))
        def _():
            pl.semaphore_wait(ready.at[d, s], 1)
            for copy in copies:
                copy.start()

    told(1, 1, first[1][1])
    for s in (1, 0):
        told(0, s, first[0][s])

    for g in range(groups):
        along_z(g, set_dz, None, ())

    for copy in loads[2:5]:
        copy.wait()
    half = 0.5 * step_size
    for p in (0, cx - 1):
        wet = jnp.where(mask_v[p] != 0, half, 0.0)
        for i in (0, 3):
            nx[i, p + 1] = wet * bar[i, p] * q[0, p + 1, rows, :]
    for s in range(2):
        start(plain, 0, s, has)
        start(late, 0, s, has)
    for copy in loads[5:]:
        copy.wait()
    table = 1.0 / jnp.minimum(dist_v[...], des_length)
    table = table * table * (2.0 * (2.0 * coef_prod / kappa_sq - 2.0 * coef_dest))
    table = jnp.broadcast_to(
        jnp.pad(table, (0, LANES - table.shape[0])).reshape(1, LANES), (8, LANES)
    )

    def look(p, carry):
        for t in range(tiles):
            here = slice(8 * t, 8 * t + 8)
            near[p, here, :] = jnp.take_along_axis(table, bin_v[p, here, :], axis=1)
        return carry

    lax.fori_loop(0, cx, look, 0, unroll=4)

    def extract(value, count, dst, base=0):
        def body(p, carry):
            for f in range(count):
                set_parts(f, p, value(f, p))
            return carry

        lax.fori_loop(0, cx, body, 0, unroll=4)
        for g in range(groups):
            along_z(g, None, dst, (0, 1), count, base)

    def wet_bar(f, p):
        return jnp.where(mask_v[p] != 0, half, 0.0) * bar[f, p]

    def own_value(f, p):
        if f == 0:
            return wet_bar(3, p) * q[3, p + 1, rows, :] * (0.5 * coef_prod)
        return dz[f - 1, p]

    above, below = pl.ds(PAD + 1, cy), pl.ds(PAD - 1, cy)

    def cross_value(f, p):
        if f == 0:
            return q[2, p + 2, rows, :] - q[2, p, rows, :]
        if f == 1:
            return q[2, p + 1, above, :] - q[2, p + 1, below, :]
        return (q[0, p + 1, above, :] - q[0, p + 1, below, :]) - (
            q[1, p + 2, rows, :] - q[1, p, rows, :]
        )

    extract(lambda f, p: wet_bar(f, p) * q[2, p + 1, rows, :], 4, own)
    extract(own_value, 3, own, 4 * groups)
    for s in range(2):
        start(middle, 2, s, greeted)

    for d in (1, 0):
        for side in range(2):
            arrive(first, d, side)
    extract(cross_value, 3, cross)
    for s in range(2):
        start(second, 2, s, greeted)
    told(2, 1, first[2][1] + middle[2][1] + second[2][1])

    def z_flux(side):
        take = lambda ref, f, base=0: ref[side, pl.ds(base + f, groups, stride=4), :]
        sign = (1.0, -1.0)[side]
        more = 4 * groups
        spin_02, spin_12 = [
            take(own_recv, 1 + f, more) + sign * take(z_send, f) - take(cross_recv, f)
            for f in range(2)
        ]
        spin_01 = take(cross_recv, 2)
        total = 1.0 + 0.25 * (spin_01 * spin_01 + spin_02 * spin_02 + spin_12 * spin_12)
        weight = take(own_recv, 0, more) * lax.rsqrt(total)
        turns = (weight * spin_02, weight * spin_12, 0.0, 0.0)
        for f in range(4):
            w_recv[side, pl.ds(f, groups, stride=4), :] = take(own_recv, f) - turns[f]

    for side in range(2):
        @pl.when(has[2][side])
        def _():
            arrive(first, 2, side)
            for g in (0, groups - 1):
                add_halo(g, z_recv, add_dz, (side,))

    def plane(p, carry, inner=True):
        along = [[] for _ in range(4)]
        for t in range(tiles):
            lo = 8 * t
            mid = slice(PAD + lo, PAD + lo + 8)
            up = slice(PAD + lo + 1, PAD + lo + 9)
            down = slice(PAD + lo - 1, PAD + lo + 7)
            here = slice(lo, lo + 8)
            cell = [q[f, p + 1, mid, :] for f in range(4)]
            diff = [
                [
                    q[f, p + 2, mid, :] - q[f, p, mid, :],
                    q[f, p + 1, up, :] - q[f, p + 1, down, :],
                    dz[f, p, here, :],
                ]
                for f in range(4)
            ]
            wet = jnp.where(mask_v[p, here, :] != 0, half, 0.0)
            bars = [bar[i, p, here, :] for i in range(4)]
            scaled = [wet * b for b in bars]
            spin = {
                (0, 1): diff[0][1] - diff[1][0],
                (0, 2): diff[0][2] - diff[2][0],
                (1, 2): diff[1][2] - diff[2][1],
            }
            total = 1.0 + 0.25 * (
                spin[0, 1] * spin[0, 1] + spin[0, 2] * spin[0, 2] + spin[1, 2] * spin[1, 2]
            )
            inverse = lax.rsqrt(total)
            omega = total * inverse
            weight = scaled[3] * cell[3] * inverse * (0.5 * coef_prod)
            flux = [[scaled[i] * cell[j] for j in range(3)] for i in range(4)]
            for (i, j), value in spin.items():
                turn = weight * value
                flux[i][j] = flux[i][j] - turn
                flux[j][i] = flux[j][i] + turn
            for i in range(4):
                if i in (1, 2) or inner:
                    nx[i, p + 1, here, :] = flux[i][0]
                ny[i, p, mid, :] = flux[i][1]
                along[i].append(flux[i][2])
            for j in range(3):
                value = bars[j]
                for i in range(4):
                    value = value - scaled[i] * diff[i][j]
                ovel[j, p, here, :] = value
            onut[p, here, :] = bars[3] + scaled[3] * (
                (2.0 * coef_prod) * omega + cell[3] * near[p, here, :]
            )
        for i in range(4):
            set_parts(i, p, jnp.concatenate(along[i], axis=0))
        return carry

    plane(0, 0, False)
    plane(cx - 1, 0, False)
    for s in range(2):
        start(second, 0, s, has)
    for side in range(2):
        @pl.when(has[2][side])
        def _():
            for g in range(1, groups - 1):
                add_halo(g, z_recv, add_dz, (side,))

    lax.fori_loop(1, cx - 1, plane, 0)
    for s in range(2):
        start(second, 1, s, has)
    for g in range(groups):
        along_z(g, add_res, None, ())

    for i in range(4):
        ny[i, :, PAD - 1, :] = jnp.zeros((cx, LANES), f32)
        ny[i, :, PAD + cy, :] = jnp.zeros((cx, LANES), f32)

    def finish(p, carry):
        for t in range(tiles):
            lo = 8 * t
            here = slice(lo, lo + 8)
            up = slice(PAD + lo + 1, PAD + lo + 9)
            down = slice(PAD + lo - 1, PAD + lo + 7)
            for i in range(4):
                value = (nx[i, p + 2, here, :] - nx[i, p, here, :]) + (
                    ny[i, p, up, :] - ny[i, p, down, :]
                )
                if i < 3:
                    ovel[i, p, here, :] += value
                else:
                    onut[p, here, :] += value
        return carry

    lax.fori_loop(1, cx - 1, finish, 0, unroll=2)
    for side in range(2):
        arrive(late, 0, side)
        arrive(plain, 0, side)
        arrive(second, 1, side)
    for s in range(2):
        p = (0, cx - 1)[s]
        wet = jnp.where(mask_v[p] != 0, (half, -half)[s], 0.0)
        ovel[0, p] += wet * (bar[0, p] * x_halo[s, 0] + bar[3, p] * x_halo[s, 1])
    for i in range(3):
        ovel[i, :, 0, :] -= y_halo[0, i]
        ovel[i, :, cy - 1, :] += y_halo[1, i]
    onut[:, 0, :] -= y_halo[0, 3]
    onut[:, cy - 1, :] += y_halo[1, 3]
    for d in range(3):
        sent(first, d)
        sent(second, d)
    sent(middle, 2)
    sent(late, 0)
    sent(plain, 0)
    def end_x():
        for side in range(2):
            arrive(second, 0, side)
        finish(0, 0)
        finish(cx - 1, 0)

    def end_z():
        for side in range(2):
            @pl.when(has[2][side])
            def _():
                arrive(middle, 2, side)
                arrive(second, 2, side)
                z_flux(side)

        for g in range(groups):
            add_halo(g, w_recv, add_res, (0, 1))

    @pl.when(first_of_run)
    def _():
        end_z()
        end_x()

    @pl.when(not_(first_of_run))
    def _():
        end_x()
        end_z()


def out_kernel(vel_in, nut_in, vel_out, nut_out, sem):
    copies = [
        pltpu.make_async_copy(vel_in, vel_out, sem.at[0]),
        pltpu.make_async_copy(nut_in, nut_out, sem.at[1]),
    ]
    for copy in copies:
        copy.start()
    for copy in copies:
        copy.wait()


def shards(counts, *args):
    velocity, nut_field = args[0], args[1]
    cx, cy, cz = nut_field.shape
    f32 = jnp.float32
    group = LANES // cy
    packed = (2, 4 * (cx // group), LANES)
    hbm = pl.BlockSpec(memory_space=pltpu.HBM)
    vmem = pl.BlockSpec(memory_space=pltpu.VMEM)
    result = pl.pallas_call(
        functools.partial(section_kernel, counts),
        out_shape=(
            jax.ShapeDtypeStruct(velocity.shape, f32),
            jax.ShapeDtypeStruct(nut_field.shape, f32),
        ),
        in_specs=[hbm] * 7,
        out_specs=(vmem, vmem),
        scratch_shapes=[
            pltpu.VMEM((4, cx + 2, cy + 2 * PAD, cz), f32),
            pltpu.VMEM((4, cx, cy, cz), f32),
            pltpu.VMEM((cx, cy, cz), jnp.int32),
            pltpu.VMEM((cx, cy, cz), jnp.int32),
            pltpu.VMEM(args[6].shape, f32),
            pltpu.VMEM((cx, cy, cz), f32),
            pltpu.VMEM((4, cx, cy, cz), f32),
            pltpu.VMEM((4, cx + 2, cy, cz), f32),
            pltpu.VMEM((4, cx, cy + 2 * PAD, cz), f32),
            pltpu.VMEM((cx * cy, 8 * LANES), jnp.bfloat16),
            pltpu.VMEM((4, 2 * LANES, 2 * LANES), jnp.bfloat16),
            pltpu.VMEM((16, 4 * LANES), jnp.bfloat16),
            pltpu.VMEM((2, 4, cx, cz), f32),
            pltpu.VMEM((2, 2, cy, cz), f32),
            pltpu.VMEM(packed, f32),
            pltpu.VMEM(packed, f32),
            pltpu.VMEM(packed, f32),
            pltpu.VMEM((2, 2 * packed[1], LANES), f32),
            pltpu.VMEM((2, 2 * packed[1], LANES), f32),
            pltpu.VMEM(packed, f32),
            pltpu.VMEM(packed, f32),
            pltpu.SemaphoreType.DMA((7,)),
            pltpu.SemaphoreType.DMA((24,)),
            pltpu.SemaphoreType.DMA((24,)),
            pltpu.SemaphoreType.REGULAR((3, 2)),
        ],
        compiler_params=pltpu.CompilerParams(
            collective_id=0, has_side_effects=True, vmem_limit_bytes=32 * 1024 * 1024
        ),
        name="section_adjoint",
    )(*[pltpu.with_memory_space_constraint(x, pltpu.HBM) for x in args])
    return pl.pallas_call(
        out_kernel,
        out_shape=(
            jax.ShapeDtypeStruct(velocity.shape, f32),
            jax.ShapeDtypeStruct(nut_field.shape, f32),
        ),
        in_specs=[vmem] * 2,
        out_specs=(hbm, hbm),
        scratch_shapes=[pltpu.SemaphoreType.DMA((2,))],
        name="section_result",
    )(*[pltpu.with_memory_space_constraint(x, pltpu.VMEM) for x in result])


def solution(mesh):
    counts = tuple(mesh.shape[a] for a in AXES)
    field = P("gx", "gy", "gz")
    tensor = P(None, "gx", "gy", "gz")
    return jax.shard_map(
        functools.partial(shards, counts),
        mesh=mesh,
        in_specs=(tensor, field, tensor, field, field, field, P()),
        out_specs=(tensor, field),
        check_vma=False,
    )
```

```python
import functools

import jax
import jax.numpy as jnp
from jax import lax
from jax.experimental import pallas as pl
from jax.experimental.pallas import tpu as pltpu
from jax.sharding import PartitionSpec as P

des_length = 0.65
step_size = 0.25
kappa_sq = 0.1681
coef_prod = 0.1355
coef_dest = 3.239

MESH = pl.DeviceIdType.MESH
AXES = ("gx", "gy", "gz")
RUN = 4
PAD = 8
LANES = 128


def section_kernel(
    counts, vel, nut, bvel, bnut, bins, mask, dist, ovel, onut,
    q, bar, bin_v, mask_v, dist_v, near, dz, nx, ny, parts, pick, place, y_halo,
    x_halo, z_send, z_recv, w_recv, own, own_recv, cross, cross_recv,
    load_sem, send_sem, recv_sem, ready,
):
    cx, cy = nut.shape[0], nut.shape[1]
    tiles = cy // 8
    group = LANES // cy
    groups = cx // group
    rows = pl.ds(PAD, cy)
    planes = pl.ds(1, cx)
    f32, bf16 = jnp.float32, jnp.bfloat16

    pos = [lax.axis_index(a) for a in AXES]
    has = [(pos[d] > 0, pos[d] < counts[d] - 1) for d in range(3)]
    peer = [({AXES[d]: pos[d] - 1}, {AXES[d]: pos[d] + 1}) for d in range(3)]

    barrier = pltpu.get_barrier_semaphore()
    first_of_run = lax.rem(pos[0], RUN) == 0
    last_of_run = lax.rem(pos[0], RUN) == RUN - 1
    upper = 2 * pos[2] >= counts[2]
    upper_low = 2 * (pos[2] - 1) >= counts[2]
    not_ = jnp.logical_not
    greeted = [
        (has[0][0] & (not_(first_of_run) | upper), has[0][1] & (last_of_run | upper)),
        (has[1][0], has[1][1] & upper),
        (has[2][0], has[2][1] & upper),
    ]
    greets = [
        (has[0][0] & (first_of_run | upper), has[0][1] & (not_(last_of_run) | upper)),
        (has[1][0] & upper, has[1][1]),
        (has[2][0] & upper_low, has[2][1]),
    ]
    for d in range(3):
        for s in range(2):
            @pl.when(greets[d][s])
            def _():
                pl.semaphore_signal(barrier, inc=1, device_id=peer[d][s], device_id_type=MESH)

    loads = [
        pltpu.make_async_copy(vel, q.at[0:3, planes, rows, :], load_sem.at[0]),
        pltpu.make_async_copy(nut, q.at[3, planes, rows, :], load_sem.at[1]),
        pltpu.make_async_copy(bvel, bar.at[0:3], load_sem.at[2]),
        pltpu.make_async_copy(bnut, bar.at[3], load_sem.at[3]),
        pltpu.make_async_copy(mask, mask_v, load_sem.at[4]),
        pltpu.make_async_copy(bins, bin_v, load_sem.at[5]),
        pltpu.make_async_copy(dist, dist_v, load_sem.at[6]),
    ]
    for copy in loads[:2]:
        copy.start()

    def remote(src, dst, slot, d, s):
        return pltpu.make_async_remote_copy(
            src_ref=src, dst_ref=dst, send_sem=send_sem.at[slot], recv_sem=recv_sem.at[slot],
            device_id=peer[d][s], device_id_type=MESH,
        )

    first = [[None, None] for _ in range(3)]
    late = [[None, None]]
    plain = [[None, None]]
    for s in range(2):
        end = (0, cx - 1)[s]
        halo = (cx + 1, 0)[s]
        first[0][s] = [remote(vel.at[1:3, end], q.at[1:3, halo, rows, :], 0 + s, 0, s)]
        late[0][s] = [
            remote(vel.at[0, end], x_halo.at[1 - s, 0], 2 + s, 0, s),
            remote(nut.at[end], x_halo.at[1 - s, 1], 16 + s, 0, s),
        ]
        end = (0, cy - 1)[s]
        halo = (PAD + cy, PAD - 1)[s]
        first[1][s] = [
            remote(vel.at[:, :, end, :], q.at[0:3, planes, halo, :], 4 + s, 1, s),
            remote(nut.at[:, end, :], q.at[3, planes, halo, :], 6 + s, 1, s),
        ]
        first[2][s] = [remote(z_send.at[s], z_recv.at[1 - s], 8 + s, 2, s)]
    middle = [None, None, [None, None]]
    second = [[None, None] for _ in range(3)]
    for s in range(2):
        end = (1, cx)[s]
        halo = (cx + 1, 0)[s]
        plain[0][s] = [
            remote(nx.at[0, end], nx.at[0, halo], 18 + s, 0, s),
            remote(nx.at[3, end], nx.at[3, halo], 20 + s, 0, s),
        ]
        second[0][s] = [remote(nx.at[1:3, end], nx.at[1:3, halo], 10 + s, 0, s)]
        end = (PAD, PAD + cy - 1)[s]
        second[1][s] = [remote(ny.at[:, :, end, :], y_halo.at[1 - s], 12 + s, 1, s)]
        middle[2][s] = [remote(own.at[s], own_recv.at[1 - s], 22 + s, 2, s)]
        second[2][s] = [remote(cross.at[s], cross_recv.at[1 - s], 14 + s, 2, s)]

    def start(copies, d, s, where):
        @pl.when(where[d][s])
        def _():
            for copy in copies[d][s]:
                copy.start()

    def arrive(copies, d, side):
        @pl.when(has[d][side])
        def _():
            for copy in copies[d][1 - side]:
                copy.wait_recv()

    def sent(copies, d):
        for s in range(2):
            @pl.when(has[d][s])
            def _():
                for copy in copies[d][s]:
                    copy.wait_send()

    for f in (0, 3):
        for halo in (0, cx + 1):
            q[f, halo, rows, :] = jnp.zeros((cy, LANES), f32)
    for s in range(2):
        @pl.when(jnp.logical_not(has[0][s]))
        def _():
            halo = (0, cx + 1)[s]
            q[1:3, halo, rows, :] = jnp.zeros((2, cy, LANES), f32)
            x_halo[s] = jnp.zeros((2, cy, LANES), f32)
            nx[:, halo] = jnp.zeros((4, cy, LANES), f32)

        @pl.when(jnp.logical_not(has[1][s]))
        def _():
            halo = (PAD - 1, PAD + cy)[s]
            for f in range(4):
                q[f, planes, halo, :] = jnp.zeros((cx, LANES), f32)
            y_halo[s] = jnp.zeros((4, cx, LANES), f32)

        @pl.when(jnp.logical_not(has[2][s]))
        def _():
            w_recv[s] = jnp.zeros((4 * groups, LANES), f32)

    at = lax.broadcasted_iota(jnp.int32, (LANES, LANES), 0)
    to = lax.broadcasted_iota(jnp.int32, (LANES, LANES), 1)
    one = lambda where: jnp.where(where, 1.0, 0.0)
    change = (one(at == to + 1) - one(at == to - 1)).astype(bf16)
    for f in range(4):
        ends = one((at == LANES - 1) & (to == f)) + one((at == 0) & (to == 4 + f))
        for half_of in range(2):
            block = pl.ds(half_of * LANES, LANES)
            pick[f, block, 0:LANES] = change
            pick[f, block, LANES:2 * LANES] = ends.astype(bf16)
    at = lax.broadcasted_iota(jnp.int32, (16, LANES), 0) % 8
    to = lax.broadcasted_iota(jnp.int32, (16, LANES), 1)
    for f in range(4):
        place[:, f * LANES:(f + 1) * LANES] = (
            one((at == 4 + f) & (to == LANES - 1)) - one((at == f) & (to == 0))
        ).astype(bf16)

    def split(value):
        coarse = value.astype(bf16)
        return coarse, (value - coarse.astype(f32)).astype(bf16)

    def set_parts(f, p, value):
        coarse, fine = split(value)
        here = pl.ds(pl.multiple_of(p * cy, cy), cy)
        parts[here, 2 * f * LANES:(2 * f + 1) * LANES] = coarse
        parts[here, (2 * f + 1) * LANES:(2 * f + 2) * LANES] = fine

    def along_z(g, take, dst, sides, count=4, base=0):
        here = pl.ds(g * LANES, LANES)
        ends = None
        for f in range(count):
            part = parts[here, 2 * f * LANES:(2 * f + 2) * LANES]
            if take is None:
                out = jnp.dot(part, pick[f, :, LANES:], preferred_element_type=f32)
            elif not sides:
                out = jnp.dot(part, pick[f, :, :LANES], preferred_element_type=f32)
                take(f, g, out.reshape(group, cy, LANES))
                continue
            else:
                out = jnp.dot(part, pick[f], preferred_element_type=f32)
                take(f, g, out[:, :LANES].reshape(group, cy, LANES))
                out = out[:, LANES:]
            ends = out if ends is None else ends + out
        if not sides:
            return
        turned = ends.T
        at_row = base + 4 * g
        for s in sides:
            dst[s, at_row:at_row + 4, :] = (turned[4:8], turned[0:4])[s]

    def add_halo(g, src, take, sides):
        value = jnp.concatenate(
            [
                src[s, 4 * g:4 * g + 4, :] if s in sides else jnp.zeros((4, LANES), f32)
                for s in range(2)
            ],
            axis=0,
        )
        coarse = value.astype(bf16).astype(f32)
        both = jnp.concatenate([coarse, value - coarse], axis=0).T.astype(bf16)
        out = jnp.dot(both, place[...], preferred_element_type=f32)
        for f in range(4):
            take(f, g, out[:, f * LANES:(f + 1) * LANES].reshape(group, cy, LANES))

    def set_dz(f, g, value):
        dz[f, g * group:(g + 1) * group] = value

    def add_dz(f, g, value):
        dz[f, g * group:(g + 1) * group] += value

    def add_res(f, g, value):
        if f < 3:
            ovel[f, g * group:(g + 1) * group] += value
        else:
            onut[g * group:(g + 1) * group] += value

    present = sum(g.astype(jnp.int32) for pair in greeted for g in pair)

    @pl.when(present > 0)
    def _():
        pl.semaphore_wait(barrier, present)

    for d in (2, 0, 1):
        for s in range(2):
            @pl.when(greeted[d][s] & not_(greets[d][s]))
            def _():
                pl.semaphore_signal(
                    ready.at[d, 1 - s], inc=1, device_id=peer[d][s], device_id_type=MESH
                )
    for s in range(2):
        start(first, 0, s, greeted)
    for s in range(2):
        start(first, 1, s, greeted)

    loads[0].wait()
    loads[1].wait()
    for copy in loads[2:]:
        copy.start()

    def part_plane(p, carry):
        for f in range(4):
            set_parts(f, p, q[f, p + 1, rows, :])
        return carry

    lax.fori_loop(0, cx, part_plane, 0, unroll=4)
    for g in range(groups):
        along_z(g, None, z_send, (0, 1))

    for s in range(2):
        start(first, 2, s, greeted)

    def told(d, s, copies):
        @pl.when(has[d][s] & not_(greeted[d][s]))
        def _():
            pl.semaphore_wait(ready.at[d, s], 1)
            for copy in copies:
                copy.start()

    told(1, 1, first[1][1])
    for s in (1, 0):
        told(0, s, first[0][s])

    for g in range(groups):
        along_z(g, set_dz, None, ())

    for copy in loads[2:5]:
        copy.wait()
    half = 0.5 * step_size
    for p in (0, cx - 1):
        wet = jnp.where(mask_v[p] != 0, half, 0.0)
        for i in (0, 3):
            nx[i, p + 1] = wet * bar[i, p] * q[0, p + 1, rows, :]
    for s in range(2):
        start(plain, 0, s, has)
        start(late, 0, s, has)
    for copy in loads[5:]:
        copy.wait()
    table = 1.0 / jnp.minimum(dist_v[...], des_length)
    table = table * table * (2.0 * (2.0 * coef_prod / kappa_sq - 2.0 * coef_dest))
    table = jnp.broadcast_to(
        jnp.pad(table, (0, LANES - table.shape[0])).reshape(1, LANES), (8, LANES)
    )

    def look(p, carry):
        for t in range(tiles):
            here = slice(8 * t, 8 * t + 8)
            near[p, here, :] = jnp.take_along_axis(table, bin_v[p, here, :], axis=1)
        return carry

    lax.fori_loop(0, cx, look, 0, unroll=4)

    def extract(value, count, dst, base=0):
        def body(p, carry):
            for f in range(count):
                set_parts(f, p, value(f, p))
            return carry

        lax.fori_loop(0, cx, body, 0, unroll=4)
        for g in range(groups):
            along_z(g, None, dst, (0, 1), count, base)

    def wet_bar(f, p):
        return jnp.where(mask_v[p] != 0, half, 0.0) * bar[f, p]

    def own_value(f, p):
        if f == 0:
            return wet_bar(3, p) * q[3, p + 1, rows, :] * (0.5 * coef_prod)
        return dz[f - 1, p]

    above, below = pl.ds(PAD + 1, cy), pl.ds(PAD - 1, cy)

    def cross_value(f, p):
        if f == 0:
            return q[2, p + 2, rows, :] - q[2, p, rows, :]
        if f == 1:
            return q[2, p + 1, above, :] - q[2, p + 1, below, :]
        return (q[0, p + 1, above, :] - q[0, p + 1, below, :]) - (
            q[1, p + 2, rows, :] - q[1, p, rows, :]
        )

    extract(lambda f, p: wet_bar(f, p) * q[2, p + 1, rows, :], 4, own)
    extract(own_value, 3, own, 4 * groups)
    for s in range(2):
        start(middle, 2, s, greeted)

    for d in (1, 0):
        for side in range(2):
            arrive(first, d, side)
    extract(cross_value, 3, cross)
    for s in range(2):
        start(second, 2, s, greeted)
    told(2, 1, first[2][1] + middle[2][1] + second[2][1])

    def z_flux(side):
        take = lambda ref, f, base=0: ref[side, pl.ds(base + f, groups, stride=4), :]
        sign = (1.0, -1.0)[side]
        more = 4 * groups
        spin_02, spin_12 = [
            take(own_recv, 1 + f, more) + sign * take(z_send, f) - take(cross_recv, f)
            for f in range(2)
        ]
        spin_01 = take(cross_recv, 2)
        total = 1.0 + 0.25 * (spin_01 * spin_01 + spin_02 * spin_02 + spin_12 * spin_12)
        weight = take(own_recv, 0, more) * lax.rsqrt(total)
        turns = (weight * spin_02, weight * spin_12, 0.0, 0.0)
        for f in range(4):
            w_recv[side, pl.ds(f, groups, stride=4), :] = take(own_recv, f) - turns[f]

    for side in range(2):
        @pl.when(has[2][side])
        def _():
            arrive(first, 2, side)
            for g in (0, groups - 1):
                add_halo(g, z_recv, add_dz, (side,))

    def plane(p, carry, inner=True):
        along = [[] for _ in range(4)]
        for t in range(tiles):
            lo = 8 * t
            mid = slice(PAD + lo, PAD + lo + 8)
            up = slice(PAD + lo + 1, PAD + lo + 9)
            down = slice(PAD + lo - 1, PAD + lo + 7)
            here = slice(lo, lo + 8)
            cell = [q[f, p + 1, mid, :] for f in range(4)]
            diff = [
                [
                    q[f, p + 2, mid, :] - q[f, p, mid, :],
                    q[f, p + 1, up, :] - q[f, p + 1, down, :],
                    dz[f, p, here, :],
                ]
                for f in range(4)
            ]
            wet = jnp.where(mask_v[p, here, :] != 0, half, 0.0)
            bars = [bar[i, p, here, :] for i in range(4)]
            scaled = [wet * b for b in bars]
            spin = {
                (0, 1): diff[0][1] - diff[1][0],
                (0, 2): diff[0][2] - diff[2][0],
                (1, 2): diff[1][2] - diff[2][1],
            }
            total = 1.0 + 0.25 * (
                spin[0, 1] * spin[0, 1] + spin[0, 2] * spin[0, 2] + spin[1, 2] * spin[1, 2]
            )
            inverse = lax.rsqrt(total)
            omega = total * inverse
            weight = scaled[3] * cell[3] * inverse * (0.5 * coef_prod)
            flux = [[scaled[i] * cell[j] for j in range(3)] for i in range(4)]
            for (i, j), value in spin.items():
                turn = weight * value
                flux[i][j] = flux[i][j] - turn
                flux[j][i] = flux[j][i] + turn
            for i in range(4):
                if i in (1, 2) or inner:
                    nx[i, p + 1, here, :] = flux[i][0]
                ny[i, p, mid, :] = flux[i][1]
                along[i].append(flux[i][2])
            for j in range(3):
                value = bars[j]
                for i in range(4):
                    value = value - scaled[i] * diff[i][j]
                ovel[j, p, here, :] = value
            onut[p, here, :] = bars[3] + scaled[3] * (
                (2.0 * coef_prod) * omega + cell[3] * near[p, here, :]
            )
        for i in range(4):
            set_parts(i, p, jnp.concatenate(along[i], axis=0))
        return carry

    plane(0, 0, False)
    plane(cx - 1, 0, False)
    for s in range(2):
        start(second, 0, s, has)
    for side in range(2):
        @pl.when(has[2][side])
        def _():
            for g in range(1, groups - 1):
                add_halo(g, z_recv, add_dz, (side,))

    lax.fori_loop(1, cx - 1, plane, 0)
    for s in range(2):
        start(second, 1, s, has)
    for g in range(groups):
        along_z(g, add_res, None, ())

    for i in range(4):
        ny[i, :, PAD - 1, :] = jnp.zeros((cx, LANES), f32)
        ny[i, :, PAD + cy, :] = jnp.zeros((cx, LANES), f32)

    def finish(p, carry):
        for t in range(tiles):
            lo = 8 * t
            here = slice(lo, lo + 8)
            up = slice(PAD + lo + 1, PAD + lo + 9)
            down = slice(PAD + lo - 1, PAD + lo + 7)
            for i in range(4):
                value = (nx[i, p + 2, here, :] - nx[i, p, here, :]) + (
                    ny[i, p, up, :] - ny[i, p, down, :]
                )
                if i < 3:
                    ovel[i, p, here, :] += value
                else:
                    onut[p, here, :] += value
        return carry

    lax.fori_loop(1, cx - 1, finish, 0, unroll=2)
    for side in range(2):
        arrive(late, 0, side)
        arrive(plain, 0, side)
        arrive(second, 1, side)
    for s in range(2):
        p = (0, cx - 1)[s]
        wet = jnp.where(mask_v[p] != 0, (half, -half)[s], 0.0)
        ovel[0, p] += wet * (bar[0, p] * x_halo[s, 0] + bar[3, p] * x_halo[s, 1])
    for i in range(3):
        ovel[i, :, 0, :] -= y_halo[0, i]
        ovel[i, :, cy - 1, :] += y_halo[1, i]
    onut[:, 0, :] -= y_halo[0, 3]
    onut[:, cy - 1, :] += y_halo[1, 3]
    for d in range(3):
        sent(first, d)
        sent(second, d)
    sent(middle, 2)
    sent(late, 0)
    sent(plain, 0)
    def end_x():
        for side in range(2):
            arrive(second, 0, side)
        finish(0, 0)
        finish(cx - 1, 0)

    def end_z():
        for side in range(2):
            @pl.when(has[2][side])
            def _():
                arrive(middle, 2, side)
                arrive(second, 2, side)
                z_flux(side)

        for g in range(groups):
            add_halo(g, w_recv, add_res, (0, 1))

    @pl.when(first_of_run)
    def _():
        end_z()
        end_x()

    @pl.when(not_(first_of_run))
    def _():
        end_x()
        end_z()


def out_kernel(vel_in, nut_in, vel_out, nut_out, sem):
    copies = [
        pltpu.make_async_copy(vel_in, vel_out, sem.at[0]),
        pltpu.make_async_copy(nut_in, nut_out, sem.at[1]),
    ]
    for copy in copies:
        copy.start()
    for copy in copies:
        copy.wait()


def shards(counts, *args):
    velocity, nut_field = args[0], args[1]
    cx, cy, cz = nut_field.shape
    f32 = jnp.float32
    group = LANES // cy
    packed = (3, 4 * (cx // group), LANES)
    hbm = pl.BlockSpec(memory_space=pltpu.HBM)
    vmem = pl.BlockSpec(memory_space=pltpu.VMEM)
    result = pl.pallas_call(
        functools.partial(section_kernel, counts),
        out_shape=(
            jax.ShapeDtypeStruct(velocity.shape, f32),
            jax.ShapeDtypeStruct(nut_field.shape, f32),
        ),
        in_specs=[hbm] * 7,
        out_specs=(vmem, vmem),
        scratch_shapes=[
            pltpu.VMEM((4, cx + 2, cy + 2 * PAD, cz), f32),
            pltpu.VMEM((4, cx, cy, cz), f32),
            pltpu.VMEM((cx, cy, cz), jnp.int32),
            pltpu.VMEM((cx, cy, cz), jnp.int32),
            pltpu.VMEM(args[6].shape, f32),
            pltpu.VMEM((cx, cy, cz), f32),
            pltpu.VMEM((4, cx, cy, cz), f32),
            pltpu.VMEM((4, cx + 2, cy, cz), f32),
            pltpu.VMEM((4, cx, cy + 2 * PAD, cz), f32),
            pltpu.VMEM((cx * cy, 8 * LANES), jnp.bfloat16),
            pltpu.VMEM((4, 2 * LANES, 2 * LANES), jnp.bfloat16),
            pltpu.VMEM((16, 4 * LANES), jnp.bfloat16),
            pltpu.VMEM((2, 4, cx, cz), f32),
            pltpu.VMEM((2, 2, cy, cz), f32),
            pltpu.VMEM(packed, f32),
            pltpu.VMEM(packed, f32),
            pltpu.VMEM(packed, f32),
            pltpu.VMEM((3, 2 * packed[1], LANES), f32),
            pltpu.VMEM((3, 2 * packed[1], LANES), f32),
            pltpu.VMEM(packed, f32),
            pltpu.VMEM(packed, f32),
            pltpu.SemaphoreType.DMA((7,)),
            pltpu.SemaphoreType.DMA((24,)),
            pltpu.SemaphoreType.DMA((24,)),
            pltpu.SemaphoreType.REGULAR((3, 2)),
        ],
        compiler_params=pltpu.CompilerParams(
            collective_id=0, has_side_effects=True, vmem_limit_bytes=32 * 1024 * 1024
        ),
        name="section_adjoint",
    )(*[pltpu.with_memory_space_constraint(x, pltpu.HBM) for x in args])
    return pl.pallas_call(
        out_kernel,
        out_shape=(
            jax.ShapeDtypeStruct(velocity.shape, f32),
            jax.ShapeDtypeStruct(nut_field.shape, f32),
        ),
        in_specs=[vmem] * 2,
        out_specs=(hbm, hbm),
        scratch_shapes=[pltpu.SemaphoreType.DMA((2,))],
        name="section_result",
    )(*[pltpu.with_memory_space_constraint(x, pltpu.VMEM) for x in result])


def solution(mesh):
    counts = tuple(mesh.shape[a] for a in AXES)
    field = P("gx", "gy", "gz")
    tensor = P(None, "gx", "gy", "gz")
    return jax.shard_map(
        functools.partial(shards, counts),
        mesh=mesh,
        in_specs=(tensor, field, tensor, field, field, field, P()),
        out_specs=(tensor, field),
        check_vma=False,
    )
```
